128 devices in a mesh: dp: 8 (over z, x_hi), ctx: 16 (over y, x_lo, core).
Axes of the slice: x: 4 (x_hi: 2, x_lo: 2; x = x_hi * 2 + x_lo), y: 4, z: 4, core: 2. Of those that a mesh axis runs over, the one named last changes fastest.
Arguments:
- queries: bfloat16 [16384, 4096], P(('dp', 'ctx')), may hold values from -6 to 6
- keys: bfloat16 [16384, 4096], P(('dp', 'ctx')), may hold values from -6 to 6
- values: bfloat16 [16384, 4096], P(('dp', 'ctx')), may hold values from -6 to 6
- grad_out: bfloat16 [16384, 4096], P(('dp', 'ctx')), may hold values from -6 to 6
- filter_param: float32 [16384, 4096], P(None, ('dp', 'ctx')), may hold values from -6 to 6
Outputs:
- query_grad: bfloat16 [16384, 4096], P(('dp', 'ctx'))
- key_grad: bfloat16 [16384, 4096], P(('dp', 'ctx'))
- value_grad: bfloat16 [16384, 4096], P(('dp', 'ctx'))
- filter_grad: float32 [16384, 4096], P(None, ('dp', 'ctx'))
The draws below stay inside these ranges and needn't reach their ends.
All inputs are finite; a program needn't handle non-finite values.
Results may differ from the reference program's by a relative error of at most 0.022.
Values may be sent and summed in bfloat16 or wider, within the bound.
A program may use at most 320 MiB of HBM per device.

```python
import math
import jax
import jax.numpy as jnp
from jax import lax

D = 4096
LEN = 16384


def level_of(key, shape, shards, least, largest):
    factor_of = 1.0
    for dim, shards_of in shards:
        steps = jax.random.uniform(jax.random.fold_in(jax.random.fold_in(key, 6), dim), (shards_of,), jnp.float32, least / len(shards), largest / len(shards))
        factor_of = factor_of * jnp.repeat(jnp.exp(steps), shape[dim] // shards_of).reshape((-1,) + (1,) * (len(shape) - 1 - dim))
    return factor_of


def centred(key, dims, spread, limit, cuts=(), held_as=jnp.bfloat16):
    entries = jax.random.normal(key, dims, jnp.float32) * spread
    if len(cuts) > 0:
        entries = level_of(key, dims, cuts, -0.22, 0.18) * entries
    return jnp.clip(entries, min=-limit, max=limit).astype(held_as)


def setup_inputs(seed: int = 0) -> dict:
    arg_keys = jax.random.split(jax.random.key(seed), 6)
    queries = centred(arg_keys[0], (LEN, D), 1.0, 6.0, ((0, 128),))
    keys = centred(arg_keys[1], (LEN, D), 1.0, 6.0, ((0, 128),))
    values = centred(arg_keys[2], (LEN, D), 1.0, 6.0, ((0, 128),))
    grad_out = centred(arg_keys[3], (LEN, D), 1.0, 6.0, ((0, 128),))
    filter_param = centred(arg_keys[4], (LEN, D), 1.0, 6.0, ((1, 128),), jnp.float32)
    return {"queries": queries, "keys": keys, "values": values, "grad_out": grad_out, "filter_param": filter_param}


def reference(queries, keys, values, grad_out, filter_param):
    n_fft = 2 * LEN
    scale = 1.0 / math.sqrt(LEN)
    block = 128 if D % 128 == 0 else D
    groups = D // block
    gated = (keys.astype(jnp.float32) * values.astype(jnp.float32)).astype(jnp.bfloat16)
    gated_grad = (grad_out.astype(jnp.float32) * queries.astype(jnp.float32)).astype(jnp.bfloat16)
    taps = filter_param * scale

    def split(array):
        return array.reshape(LEN, groups, block).transpose(1, 0, 2)

    def one_block(inputs):
        part_gated, part_grad, part_taps = inputs
        spectrum_gated = jnp.fft.rfft(part_gated.astype(jnp.float32), n=n_fft, axis=0)
        spectrum_grad = jnp.fft.rfft(part_grad.astype(jnp.float32), n=n_fft, axis=0)
        spectrum_taps = jnp.fft.rfft(part_taps, n=n_fft, axis=0)
        conv_out = jnp.fft.irfft(spectrum_gated * spectrum_taps, n=n_fft, axis=0)[:LEN]
        gated_back = jnp.fft.irfft(spectrum_grad * jnp.conj(spectrum_taps), n=n_fft, axis=0)[:LEN]
        cross = jnp.conj(spectrum_gated) * spectrum_grad
        filter_grad = jnp.fft.irfft(cross, n=n_fft, axis=0)[:LEN] * scale
        return (conv_out.astype(jnp.bfloat16), gated_back.astype(jnp.bfloat16), filter_grad.astype(jnp.float32))
    conv_out, gated_back, filter_grad = lax.map(one_block, (split(gated), split(gated_grad), split(taps)))
    conv_out = conv_out.transpose(1, 0, 2).reshape(LEN, D)
    gated_back = gated_back.transpose(1, 0, 2).reshape(LEN, D)
    filter_grad = filter_grad.transpose(1, 0, 2).reshape(LEN, D)
    query_grad = (grad_out.astype(jnp.float32) * conv_out.astype(jnp.float32)).astype(jnp.bfloat16)
    key_grad = (gated_back.astype(jnp.float32) * values.astype(jnp.float32)).astype(jnp.bfloat16)
    value_grad = (gated_back.astype(jnp.float32) * keys.astype(jnp.float32)).astype(jnp.bfloat16)
    return (query_grad, key_grad, value_grad, filter_grad)
```

```python
import functools
import math

import jax
import jax.numpy as jnp
import numpy as np
from jax import lax
from jax.experimental import pallas as pl
from jax.experimental.pallas import tpu as pltpu
from jax.sharding import PartitionSpec as P

MESH = pl.DeviceIdType.MESH
F32 = jnp.float32
BF16 = jnp.bfloat16
N = 128
W = 32
C = N * W
GROUP = 4


def make_tables():
    a = np.arange(128, dtype=np.float64)
    k = np.arange(128, dtype=np.float64)
    outer = 2.0 * np.pi * np.outer(k + 0.5, a) / 256.0
    first = np.concatenate([np.cos(outer), -np.sin(outer)], axis=0)
    last = first.T * (2.0 / 32768.0 / 128.0)
    inner = 2.0 * np.pi * (np.outer(a, a) % 128) / 128.0
    c, s = np.cos(inner), np.sin(inner)
    second = np.block([[c, -s], [s, c]])
    twist = 2.0 * np.pi * np.outer(k + 0.5, a) / 32768.0
    index = np.arange(256)
    swap = np.zeros((256, 256))
    swap[index, (index % 16) * 16 + index // 16] = 1.0
    wide = np.concatenate([second, second.T, np.eye(256), swap, last], axis=0)
    return (
        jnp.asarray(wide.astype(np.float32), BF16),
        jnp.asarray(first.astype(np.float32), BF16),
        jnp.asarray(np.concatenate([np.cos(twist), np.sin(twist)], axis=0), F32),
    )


def dot(x, y):
    return lax.dot_general(x, y, (((1,), (0,)), ((), ())), preferred_element_type=F32)


def dot_nt(x, y):
    return lax.dot_general(x, y, (((1,), (1,)), ((), ())), preferred_element_type=F32)


def kernel(
    q_hbm, k_hbm, v_hbm, g_hbm, taps_hbm, wide_hbm, first_hbm, twist_hbm,
    qg_ref, kg_ref, vg_ref, fg_ref,
    q, k, v, g, taps, wide, first, twist,
    send, recv, xt, spec_h, spec_g, spec_q,
    load_sem, send_sem, recv_sem, own_sem,
):
    dp, ctx = lax.axis_index("dp"), lax.axis_index("ctx")
    me = dp * 16 + ctx
    cx, cy, cz, cc = (dp % 2) * 2 + (ctx // 2) % 2, ctx // 4, dp // 2, ctx % 2

    loads = [
        pltpu.make_async_copy(src, dst, load_sem.at[i])
        for i, (src, dst) in enumerate(
            [(wide_hbm, wide), (k_hbm, k), (v_hbm, v), (q_hbm, q), (g_hbm, g),
             (first_hbm, first), (twist_hbm, twist), (taps_hbm, taps)]
        )
    ]
    for load in loads:
        load.start()

    def partner(i):
        x = (cx + i) % 4
        y = (cy + i // 4 + i) % 4
        z = (cz + i // 16 + i // 4 + i) % 4
        c = (cc + i // 64 + i) % 2
        return z * 2 + x // 2, y * 4 + (x % 2) * 2 + c

    barrier = pltpu.get_barrier_semaphore()

    @pl.loop(1, N)
    def _(i):
        pl.semaphore_signal(barrier, inc=1, device_id=partner(i), device_id_type=MESH)

    ident = wide.at[512:768]
    swap = wide.at[768:1024]

    def gate_in(left, right, slot):
        @pl.loop(0, C // 256)
        def _(i):
            cols = pl.ds(pl.multiple_of(i * 256, 256), 256)
            gated = (left[:, cols].astype(F32) * right[:, cols].astype(F32)).astype(BF16)
            turned = dot_nt(ident[...], gated).astype(BF16)
            send[slot, pl.ds(pl.multiple_of(i * 8, 8), 8)] = turned.reshape(8, W, 128)

    for load in loads[:3]:
        load.wait()
    gate_in(k, v, 0)
    for load in loads[3:5]:
        load.wait()
    gate_in(g, q, 1)
    pl.semaphore_wait(barrier, N - 1)

    def start_sends(slot):
        @pl.loop(1, N)
        def _(i):
            d, e = partner(i)
            pltpu.make_async_remote_copy(
                src_ref=send.at[slot, d * 16 + e],
                dst_ref=recv.at[slot, me],
                send_sem=send_sem.at[slot],
                recv_sem=recv_sem.at[slot],
                device_id=(d, e),
                device_id_type=MESH,
            ).start()

        pltpu.make_async_copy(send.at[slot, me], recv.at[slot, me], own_sem.at[slot]).start()

    def wait_recv(slot):
        others = recv.at[slot, pl.ds(0, N - 1)]
        pltpu.make_async_copy(others, others, recv_sem.at[slot]).wait()
        pltpu.make_async_copy(send.at[slot, me], recv.at[slot, me], own_sem.at[slot]).wait()

    def wait_send(slot):
        others = send.at[slot, pl.ds(0, N - 1)]
        pltpu.make_async_copy(others, others, send_sem.at[slot]).wait()

    start_sends(0)
    start_sends(1)
    for load in loads[5:]:
        load.wait()

    cos, sin = twist.at[0:128], twist.at[128:256]

    def swap_blocks(load_block, store_block):
        @pl.loop(0, 8)
        def _(i):
            for j in range(2):
                store_block(i, j, dot(swap[...], load_block(i, j)))

    def recv_block(slot):
        def load(i, j):
            rows = recv[slot, pl.ds(pl.multiple_of(i * 16, 16), 16), pl.ds(j * 16, 16), :]
            return rows.reshape(256, 128)

        return load

    def taps_block(i, j):
        parts = []
        for s in range(16):
            lanes = pl.ds(pl.multiple_of((i * 16 + s) * 128, 128), 128)
            parts.append(taps[pl.ds(j * 16, 16), lanes])
        return jnp.concatenate(parts, axis=0).astype(BF16)

    def xt_store(i, j, block):
        rows = pl.ds(pl.multiple_of(i * 16, 16), 16)
        xt[pl.ds(j * 16, 16), rows, :] = block.astype(BF16).reshape(16, 16, 128)

    def xt_block(i, j):
        rows = pl.ds(pl.multiple_of(i * 16, 16), 16)
        return xt[pl.ds(j * 16, 16), rows, :].reshape(256, 128)

    def send_store(slot):
        def store(i, j, block):
            rows = pl.ds(pl.multiple_of(i * 16, 16), 16)
            send[slot, rows, pl.ds(j * 16, 16), :] = block.astype(BF16).reshape(16, 16, 128)

        return store

    def fg_store(i, j, block):
        for s in range(16):
            lanes = pl.ds(pl.multiple_of((i * 16 + s) * 128, 128), 128)
            fg_ref[pl.ds(j * 16, 16), lanes] = block[s * 16 : (s + 1) * 16]

    def forward(ws):
        outer = [dot(first[...], xt[w]) for w in ws]
        twisted = []
        for x in outer:
            re, im = x[:128], x[128:]
            c, s = cos[...], sin[...]
            twisted.append(
                jnp.concatenate([re * c + im * s, im * c - re * s], axis=1).astype(BF16)
            )
        return [dot(x, wide[0:256]) for x in twisted]

    def backward(ws, products):
        inner = [dot(x, wide[256:512]) for x in products]
        twisted = []
        for x in inner:
            re, im = x[:, :128], x[:, 128:]
            c, s = cos[...], sin[...]
            twisted.append(
                jnp.concatenate([re * c - im * s, re * s + im * c], axis=0).astype(BF16)
            )
        for w, x in zip(ws, twisted):
            xt[w] = dot(wide[1024:1152], x).astype(BF16)

    def product(x, y):
        xr, xi, yr, yi = x[:, :128], x[:, 128:], y[:, :128], y[:, 128:]
        return jnp.concatenate([xr * yr - xi * yi, xr * yi + xi * yr], axis=1).astype(BF16)

    def conj_product(x, y):
        xr, xi, yr, yi = x[:, :128], x[:, 128:], y[:, :128], y[:, 128:]
        return jnp.concatenate([xr * yr + xi * yi, xr * yi - xi * yr], axis=1).astype(BF16)

    def groups(body):
        @pl.loop(0, W // GROUP)
        def _(i):
            body([i * GROUP + j for j in range(GROUP)])

    swap_blocks(taps_block, xt_store)

    def taps_step(ws):
        for w, x in zip(ws, forward(ws)):
            spec_h[w] = x.astype(BF16)

    groups(taps_step)

    wait_recv(0)
    swap_blocks(recv_block(0), xt_store)

    def gated_step(ws):
        found = forward(ws)
        for w, x in zip(ws, found):
            spec_g[w] = x.astype(BF16)
        backward(ws, [product(x, spec_h[w].astype(F32)) for w, x in zip(ws, found)])

    groups(gated_step)
    swap_blocks(xt_block, send_store(2))
    start_sends(2)

    wait_recv(1)
    swap_blocks(recv_block(1), xt_store)

    def grad_step(ws):
        found = forward(ws)
        for w, x in zip(ws, found):
            spec_q[w] = x.astype(BF16)
        backward(ws, [conj_product(spec_h[w].astype(F32), x) for w, x in zip(ws, found)])

    groups(grad_step)
    swap_blocks(xt_block, send_store(3))
    start_sends(3)

    def filter_step(ws):
        backward(ws, [conj_product(spec_g[w].astype(F32), spec_q[w].astype(F32)) for w in ws])

    groups(filter_step)
    swap_blocks(xt_block, fg_store)

    def turned(slot, i):
        rows = recv[slot, pl.ds(pl.multiple_of(i * 8, 8), 8)].reshape(256, 128)
        return dot_nt(wide[512:640, 0:128], rows)

    wait_recv(2)

    @pl.loop(0, C // 256)
    def _(i):
        cols = pl.ds(pl.multiple_of(i * 256, 256), 256)
        qg_ref[:, cols] = (g[:, cols].astype(F32) * turned(2, i)).astype(BF16)

    wait_recv(3)

    @pl.loop(0, C // 256)
    def _(i):
        cols = pl.ds(pl.multiple_of(i * 256, 256), 256)
        back = turned(3, i)
        kg_ref[:, cols] = (v[:, cols].astype(F32) * back).astype(BF16)
        vg_ref[:, cols] = (k[:, cols].astype(F32) * back).astype(BF16)

    for slot in range(4):
        wait_send(slot)


def local(queries, keys, values, grad_out, filter_param):
    wide, first, twist = make_tables()
    hbm = pl.BlockSpec(memory_space=pltpu.HBM)
    vmem = pl.BlockSpec(memory_space=pltpu.VMEM)
    rows = (N, C)
    out = pl.pallas_call(
        kernel,
        out_shape=[jax.ShapeDtypeStruct(rows, BF16)] * 3
        + [jax.ShapeDtypeStruct((W, N * N), F32)],
        in_specs=[hbm] * 8,
        out_specs=[vmem] * 4,
        scratch_shapes=[
            pltpu.VMEM(rows, BF16),
            pltpu.VMEM(rows, BF16),
            pltpu.VMEM(rows, BF16),
            pltpu.VMEM(rows, BF16),
            pltpu.VMEM((W, N * N), F32),
            pltpu.VMEM(wide.shape, BF16),
            pltpu.VMEM(first.shape, BF16),
            pltpu.VMEM(twist.shape, F32),
            pltpu.VMEM((4, N, W, 128), BF16),
            pltpu.VMEM((4, N, W, 128), BF16),
            pltpu.VMEM((W, 128, 128), BF16),
            pltpu.VMEM((W, 128, 256), BF16),
            pltpu.VMEM((W, 128, 256), BF16),
            pltpu.VMEM((W, 128, 256), BF16),
            pltpu.SemaphoreType.DMA((8,)),
            pltpu.SemaphoreType.DMA((4,)),
            pltpu.SemaphoreType.DMA((4,)),
            pltpu.SemaphoreType.DMA((4,)),
        ],
        compiler_params=pltpu.CompilerParams(
            collective_id=0, has_side_effects=True, vmem_limit_bytes=48 << 20
        ),
        cost_estimate=pl.CostEstimate(flops=5 << 30, bytes_accessed=11 << 20, transcendentals=0),
    )(queries, keys, values, grad_out, filter_param.T, wide, first, twist)
    query_grad, key_grad, value_grad, filter_grad = out
    return query_grad, key_grad, value_grad, filter_grad.T


def solution(mesh):
    split = P(("dp", "ctx"), None)
    channels = P(None, ("dp", "ctx"))
    return jax.shard_map(
        local,
        mesh=mesh,
        in_specs=(split, split, split, split, channels),
        out_specs=(split, split, split, channels),
        check_vma=False,
    )
```

```python
import functools
import math

import jax
import jax.numpy as jnp
import numpy as np
from jax import lax
from jax.experimental import pallas as pl
from jax.experimental.pallas import tpu as pltpu
from jax.sharding import PartitionSpec as P

MESH = pl.DeviceIdType.MESH
F32 = jnp.float32
BF16 = jnp.bfloat16
N = 128
W = 32
C = N * W
GROUP = 4
UNROLL = 4
SWAP_UNROLL = 2


def make_tables():
    a = np.arange(128, dtype=np.float64)
    k = np.arange(128, dtype=np.float64)
    outer = 2.0 * np.pi * np.outer(k + 0.5, a) / 256.0
    first = np.concatenate([np.cos(outer), -np.sin(outer)], axis=0)
    last = first.T * (2.0 / 32768.0 / 128.0)
    inner = 2.0 * np.pi * (np.outer(a, a) % 128) / 128.0
    c, s = np.cos(inner), np.sin(inner)
    second = np.block([[c, -s], [s, c]])
    twist = 2.0 * np.pi * np.outer(k + 0.5, a) / 32768.0
    index = np.arange(256)
    swap = np.zeros((256, 256))
    swap[index, (index % 16) * 16 + index // 16] = 1.0
    wide = np.concatenate([second, second.T, np.eye(256), swap, last], axis=0)
    return (
        jnp.asarray(wide.astype(np.float32), BF16),
        jnp.asarray(first.astype(np.float32), BF16),
        jnp.asarray(np.concatenate([np.cos(twist), np.sin(twist)], axis=0), F32),
    )


def dot(x, y):
    return lax.dot_general(x, y, (((1,), (0,)), ((), ())), preferred_element_type=F32)


def dot_nt(x, y):
    return lax.dot_general(x, y, (((1,), (1,)), ((), ())), preferred_element_type=F32)


def kernel(
    q_hbm, k_hbm, v_hbm, g_hbm, taps_hbm, wide_hbm, first_hbm, twist_hbm,
    qg_ref, kg_ref, vg_ref, fg_ref,
    q, k, v, g, taps, wide, first, twist,
    send, recv, xt, spec_h, spec_g, spec_q,
    load_sem, send_sem, recv_sem, own_sem,
):
    dp, ctx = lax.axis_index("dp"), lax.axis_index("ctx")
    me = dp * 16 + ctx
    cx, cy, cz, cc = (dp % 2) * 2 + (ctx // 2) % 2, ctx // 4, dp // 2, ctx % 2

    loads = [
        pltpu.make_async_copy(src, dst, load_sem.at[i])
        for i, (src, dst) in enumerate(
            [(wide_hbm, wide), (k_hbm, k), (v_hbm, v), (q_hbm, q), (g_hbm, g),
             (first_hbm, first), (twist_hbm, twist), (taps_hbm, taps)]
        )
    ]
    for load in loads:
        load.start()

    def partner(i):
        x = (cx + i) % 4
        y = (cy + i // 4 + i) % 4
        z = (cz + i // 16 + i // 4 + i) % 4
        c = (cc + i // 64 + i) % 2
        return z * 2 + x // 2, y * 4 + (x % 2) * 2 + c

    barrier = pltpu.get_barrier_semaphore()

    @pl.loop(1, N)
    def _(i):
        pl.semaphore_signal(barrier, inc=1, device_id=partner(i), device_id_type=MESH)

    ident = wide.at[512:768]
    swap = wide.at[768:1024]

    def gate_in(left, right, slot):
        @pl.loop(0, C // 256 // UNROLL)
        def _(i):
            turned = []
            for u in range(UNROLL):
                cols = pl.ds(pl.multiple_of(i * (256 * UNROLL) + u * 256, 256), 256)
                gated = (left[:, cols].astype(F32) * right[:, cols].astype(F32)).astype(BF16)
                turned.append(dot_nt(ident[...], gated).astype(BF16))
            for u in range(UNROLL):
                send[slot, pl.ds(pl.multiple_of(i * (8 * UNROLL) + u * 8, 8), 8)] = turned[u].reshape(8, W, 128)

    for load in loads[:3]:
        load.wait()
    gate_in(k, v, 0)
    pl.semaphore_wait(barrier, N - 1)

    def start_sends(slot):
        @pl.loop(1, N)
        def _(i):
            d, e = partner(i)
            pltpu.make_async_remote_copy(
                src_ref=send.at[slot, d * 16 + e],
                dst_ref=recv.at[slot, me],
                send_sem=send_sem.at[slot],
                recv_sem=recv_sem.at[slot],
                device_id=(d, e),
                device_id_type=MESH,
            ).start()

        pltpu.make_async_copy(send.at[slot, me], recv.at[slot, me], own_sem.at[slot]).start()

    def wait_recv(slot):
        others = recv.at[slot, pl.ds(0, N - 1)]
        pltpu.make_async_copy(others, others, recv_sem.at[slot]).wait()
        pltpu.make_async_copy(send.at[slot, me], recv.at[slot, me], own_sem.at[slot]).wait()

    def wait_send(slot):
        others = send.at[slot, pl.ds(0, N - 1)]
        pltpu.make_async_copy(others, others, send_sem.at[slot]).wait()

    start_sends(0)
    for load in loads[3:5]:
        load.wait()
    gate_in(g, q, 1)
    start_sends(1)
    for load in loads[5:]:
        load.wait()

    cos, sin = twist.at[0:128], twist.at[128:256]

    def swap_blocks(load_block, store_block):
        @pl.loop(0, 8 // SWAP_UNROLL)
        def _(i):
            blocks = [(i * SWAP_UNROLL + u, j) for u in range(SWAP_UNROLL) for j in range(2)]
            found = [dot(swap[...], load_block(*block)) for block in blocks]
            for block, x in zip(blocks, found):
                store_block(*block, x)

    def recv_block(slot):
        def load(i, j):
            rows = recv[slot, pl.ds(pl.multiple_of(i * 16, 16), 16), pl.ds(j * 16, 16), :]
            return rows.reshape(256, 128)

        return load

    def taps_block(i, j):
        parts = []
        for s in range(16):
            lanes = pl.ds(pl.multiple_of((i * 16 + s) * 128, 128), 128)
            parts.append(taps[pl.ds(j * 16, 16), lanes])
        return jnp.concatenate(parts, axis=0).astype(BF16)

    def xt_store(i, j, block):
        rows = pl.ds(pl.multiple_of(i * 16, 16), 16)
        xt[pl.ds(j * 16, 16), rows, :] = block.astype(BF16).reshape(16, 16, 128)

    def xt_block(i, j):
        rows = pl.ds(pl.multiple_of(i * 16, 16), 16)
        return xt[pl.ds(j * 16, 16), rows, :].reshape(256, 128)

    def send_store(slot):
        def store(i, j, block):
            rows = pl.ds(pl.multiple_of(i * 16, 16), 16)
            send[slot, rows, pl.ds(j * 16, 16), :] = block.astype(BF16).reshape(16, 16, 128)

        return store

    def fg_store(i, j, block):
        for s in range(16):
            lanes = pl.ds(pl.multiple_of((i * 16 + s) * 128, 128), 128)
            fg_ref[pl.ds(j * 16, 16), lanes] = block[s * 16 : (s + 1) * 16]

    def forward(ws):
        outer = [dot(first[...], xt[w]) for w in ws]
        twisted = []
        for x in outer:
            re, im = x[:128], x[128:]
            c, s = cos[...], sin[...]
            twisted.append(
                jnp.concatenate([re * c + im * s, im * c - re * s], axis=1).astype(BF16)
            )
        return [dot(x, wide[0:256]) for x in twisted]

    def backward(ws, products):
        inner = [dot(x, wide[256:512]) for x in products]
        twisted = []
        for x in inner:
            re, im = x[:, :128], x[:, 128:]
            c, s = cos[...], sin[...]
            twisted.append(
                jnp.concatenate([re * c - im * s, re * s + im * c], axis=0).astype(BF16)
            )
        for w, x in zip(ws, twisted):
            xt[w] = dot(wide[1024:1152], x).astype(BF16)

    def product(x, y):
        xr, xi, yr, yi = x[:, :128], x[:, 128:], y[:, :128], y[:, 128:]
        return jnp.concatenate([xr * yr - xi * yi, xr * yi + xi * yr], axis=1).astype(BF16)

    def conj_product(x, y):
        xr, xi, yr, yi = x[:, :128], x[:, 128:], y[:, :128], y[:, 128:]
        return jnp.concatenate([xr * yr + xi * yi, xr * yi - xi * yr], axis=1).astype(BF16)

    def groups(body):
        @pl.loop(0, W // GROUP)
        def _(i):
            body([i * GROUP + j for j in range(GROUP)])

    swap_blocks(taps_block, xt_store)

    def taps_step(ws):
        for w, x in zip(ws, forward(ws)):
            spec_h[w] = x.astype(BF16)

    groups(taps_step)

    wait_recv(0)
    swap_blocks(recv_block(0), xt_store)

    def gated_step(ws):
        found = forward(ws)
        for w, x in zip(ws, found):
            spec_g[w] = x.astype(BF16)
        backward(ws, [product(x, spec_h[w].astype(F32)) for w, x in zip(ws, found)])

    groups(gated_step)
    swap_blocks(xt_block, send_store(2))
    start_sends(2)

    wait_recv(1)
    swap_blocks(recv_block(1), xt_store)

    def grad_step(ws):
        found = forward(ws)
        for w, x in zip(ws, found):
            spec_q[w] = x.astype(BF16)
        backward(ws, [conj_product(spec_h[w].astype(F32), x) for w, x in zip(ws, found)])

    groups(grad_step)
    swap_blocks(xt_block, send_store(3))
    start_sends(3)

    def filter_step(ws):
        backward(ws, [conj_product(spec_g[w].astype(F32), spec_q[w].astype(F32)) for w in ws])

    groups(filter_step)
    swap_blocks(xt_block, fg_store)

    def turned(slot, i):
        rows = recv[slot, pl.ds(pl.multiple_of(i * 8, 8), 8)].reshape(256, 128)
        return dot_nt(wide[512:640, 0:128], rows)

    def gate_out(slot, pairs):
        @pl.loop(0, C // 256 // UNROLL)
        def _(i):
            found = [turned(slot, i * UNROLL + u) for u in range(UNROLL)]
            for u in range(UNROLL):
                cols = pl.ds(pl.multiple_of(i * (256 * UNROLL) + u * 256, 256), 256)
                for out_ref, gate in pairs:
                    out_ref[:, cols] = (gate[:, cols].astype(F32) * found[u]).astype(BF16)

    wait_recv(2)
    gate_out(2, [(qg_ref, g)])
    wait_recv(3)
    gate_out(3, [(kg_ref, v), (vg_ref, k)])

    for slot in range(4):
        wait_send(slot)


def local(queries, keys, values, grad_out, filter_param):
    wide, first, twist = make_tables()
    hbm = pl.BlockSpec(memory_space=pltpu.HBM)
    vmem = pl.BlockSpec(memory_space=pltpu.VMEM)
    rows = (N, C)
    out = pl.pallas_call(
        kernel,
        out_shape=[jax.ShapeDtypeStruct(rows, BF16)] * 3
        + [jax.ShapeDtypeStruct((W, N * N), F32)],
        in_specs=[hbm] * 8,
        out_specs=[vmem] * 4,
        scratch_shapes=[
            pltpu.VMEM(rows, BF16),
            pltpu.VMEM(rows, BF16),
            pltpu.VMEM(rows, BF16),
            pltpu.VMEM(rows, BF16),
            pltpu.VMEM((W, N * N), F32),
            pltpu.VMEM(wide.shape, BF16),
            pltpu.VMEM(first.shape, BF16),
            pltpu.VMEM(twist.shape, F32),
            pltpu.VMEM((4, N, W, 128), BF16),
            pltpu.VMEM((4, N, W, 128), BF16),
            pltpu.VMEM((W, 128, 128), BF16),
            pltpu.VMEM((W, 128, 256), BF16),
            pltpu.VMEM((W, 128, 256), BF16),
            pltpu.VMEM((W, 128, 256), BF16),
            pltpu.SemaphoreType.DMA((8,)),
            pltpu.SemaphoreType.DMA((4,)),
            pltpu.SemaphoreType.DMA((4,)),
            pltpu.SemaphoreType.DMA((4,)),
        ],
        compiler_params=pltpu.CompilerParams(
            collective_id=0, has_side_effects=True, vmem_limit_bytes=62 << 20
        ),
        cost_estimate=pl.CostEstimate(flops=5 << 30, bytes_accessed=11 << 20, transcendentals=0),
    )(queries, keys, values, grad_out, filter_param.T, wide, first, twist)
    query_grad, key_grad, value_grad, filter_grad = out
    return query_grad, key_grad, value_grad, filter_grad.T


def solution(mesh):
    split = P(("dp", "ctx"), None)
    channels = P(None, ("dp", "ctx"))
    return jax.shard_map(
        local,
        mesh=mesh,
        in_specs=(split, split, split, split, channels),
        out_specs=(split, split, split, channels),
        check_vma=False,
    )
```

```python
import functools
import math

import jax
import jax.numpy as jnp
import numpy as np
from jax import lax
from jax.experimental import pallas as pl
from jax.experimental.pallas import tpu as pltpu
from jax.sharding import PartitionSpec as P

MESH = pl.DeviceIdType.MESH
F32 = jnp.float32
BF16 = jnp.bfloat16
N = 128
W = 32
C = N * W
GROUP = 4
UNROLL = 4
SWAP_UNROLL = 2


def make_tables():
    a = np.arange(128, dtype=np.float64)
    k = np.arange(128, dtype=np.float64)
    outer = 2.0 * np.pi * np.outer(k + 0.5, a) / 256.0
    first = np.concatenate([np.cos(outer), -np.sin(outer)], axis=0)
    last = first.T * (2.0 / 32768.0 / 128.0)
    inner = 2.0 * np.pi * (np.outer(a, a) % 128) / 128.0
    c, s = np.cos(inner), np.sin(inner)
    second = np.block([[c, -s], [s, c]])
    twist = 2.0 * np.pi * np.outer(k + 0.5, a) / 32768.0
    index = np.arange(256)
    swap = np.zeros((256, 256))
    swap[index, (index % 16) * 16 + index // 16] = 1.0
    wide = np.concatenate([second, second.T, np.eye(256), swap, last], axis=0)
    return (
        jnp.asarray(wide.astype(np.float32), BF16),
        jnp.asarray(first.astype(np.float32), BF16),
        jnp.asarray(np.concatenate([np.cos(twist), np.sin(twist)], axis=0), F32),
    )


def dot(x, y):
    return lax.dot_general(x, y, (((1,), (0,)), ((), ())), preferred_element_type=F32)


def dot_nt(x, y):
    return lax.dot_general(x, y, (((1,), (1,)), ((), ())), preferred_element_type=F32)


def kernel(
    q_hbm, k_hbm, v_hbm, g_hbm, taps_hbm, wide_hbm, first_hbm, twist_hbm,
    qg_ref, kg_ref, vg_ref, fg_ref,
    q, k, v, g, taps, wide, first, twist,
    send, recv, xt, spec_h, spec_g, spec_q,
    load_sem, send_sem, recv_sem, own_sem,
):
    dp, ctx = lax.axis_index("dp"), lax.axis_index("ctx")
    me = dp * 16 + ctx
    cx, cy, cz, cc = (dp % 2) * 2 + (ctx // 2) % 2, ctx // 4, dp // 2, ctx % 2

    loads = [
        pltpu.make_async_copy(src, dst, load_sem.at[i])
        for i, (src, dst) in enumerate(
            [(wide_hbm, wide), (k_hbm, k), (v_hbm, v), (q_hbm, q), (g_hbm, g),
             (first_hbm, first), (twist_hbm, twist), (taps_hbm, taps)]
        )
    ]
    for load in loads:
        load.start()

    def partner(i):
        x = (cx + i) % 4
        y = (cy + i // 4 + i) % 4
        z = (cz + i // 16 + i // 4 + i) % 4
        c = (cc + i // 64 + i) % 2
        return z * 2 + x // 2, y * 4 + (x % 2) * 2 + c

    barrier = pltpu.get_barrier_semaphore()

    @pl.loop(1, N)
    def _(i):
        pl.semaphore_signal(barrier, inc=1, device_id=partner(i), device_id_type=MESH)

    ident = wide.at[512:768]
    swap = wide.at[768:1024]

    def gate_in(left, right, slot):
        @pl.loop(0, C // 256 // UNROLL)
        def _(i):
            turned = []
            for u in range(UNROLL):
                cols = pl.ds(pl.multiple_of(i * (256 * UNROLL) + u * 256, 256), 256)
                gated = (left[:, cols].astype(F32) * right[:, cols].astype(F32)).astype(BF16)
                turned.append(dot_nt(ident[...], gated).astype(BF16))
            for u in range(UNROLL):
                send[slot, pl.ds(pl.multiple_of(i * (8 * UNROLL) + u * 8, 8), 8)] = turned[u].reshape(8, W, 128)

    for load in loads[:3]:
        load.wait()
    gate_in(k, v, 0)
    pl.semaphore_wait(barrier, N - 1)

    def start_sends(slot):
        @pl.loop(1, N)
        def _(i):
            d, e = partner(i)
            pltpu.make_async_remote_copy(
                src_ref=send.at[slot, d * 16 + e],
                dst_ref=recv.at[slot, me],
                send_sem=send_sem.at[slot],
                recv_sem=recv_sem.at[slot],
                device_id=(d, e),
                device_id_type=MESH,
            ).start()

        pltpu.make_async_copy(send.at[slot, me], recv.at[slot, me], own_sem.at[slot]).start()

    def wait_recv(slot):
        others = recv.at[slot, pl.ds(0, N - 1)]
        pltpu.make_async_copy(others, others, recv_sem.at[slot]).wait()
        pltpu.make_async_copy(send.at[slot, me], recv.at[slot, me], own_sem.at[slot]).wait()

    def wait_send(slot):
        others = send.at[slot, pl.ds(0, N - 1)]
        pltpu.make_async_copy(others, others, send_sem.at[slot]).wait()

    start_sends(0)
    for load in loads[3:5]:
        load.wait()
    gate_in(g, q, 1)
    start_sends(1)
    for load in loads[5:]:
        load.wait()

    cos, sin = twist.at[0:128], twist.at[128:256]

    def swap_blocks(load_block, store_block):
        @pl.loop(0, 8 // SWAP_UNROLL)
        def _(i):
            blocks = [(i * SWAP_UNROLL + u, j) for u in range(SWAP_UNROLL) for j in range(2)]
            found = [dot(swap[...], load_block(*block)) for block in blocks]
            for block, x in zip(blocks, found):
                store_block(*block, x)

    def recv_block(slot):
        def load(i, j):
            rows = recv[slot, pl.ds(pl.multiple_of(i * 16, 16), 16), pl.ds(j * 16, 16), :]
            return rows.reshape(256, 128)

        return load

    def taps_block(i, j):
        parts = []
        for s in range(16):
            lanes = pl.ds(pl.multiple_of((i * 16 + s) * 128, 128), 128)
            parts.append(taps[pl.ds(j * 16, 16), lanes])
        return jnp.concatenate(parts, axis=0).astype(BF16)

    def xt_store(i, j, block):
        rows = pl.ds(pl.multiple_of(i * 16, 16), 16)
        xt[pl.ds(j * 16, 16), rows, :] = block.astype(BF16).reshape(16, 16, 128)

    def xt_block(i, j):
        rows = pl.ds(pl.multiple_of(i * 16, 16), 16)
        return xt[pl.ds(j * 16, 16), rows, :].reshape(256, 128)

    def send_store(slot):
        def store(i, j, block):
            rows = pl.ds(pl.multiple_of(i * 16, 16), 16)
            send[slot, rows, pl.ds(j * 16, 16), :] = block.astype(BF16).reshape(16, 16, 128)

        return store

    def fg_store(i, j, block):
        for s in range(16):
            lanes = pl.ds(pl.multiple_of((i * 16 + s) * 128, 128), 128)
            fg_ref[pl.ds(j * 16, 16), lanes] = block[s * 16 : (s + 1) * 16]

    def forward(ws):
        outer = [dot(first[...], xt[w]) for w in ws]
        twisted = []
        for x in outer:
            re, im = x[:128], x[128:]
            c, s = cos[...], sin[...]
            twisted.append(
                jnp.concatenate([re * c + im * s, im * c - re * s], axis=1).astype(BF16)
            )
        return [dot(x, wide[0:256]) for x in twisted]

    def backward(ws, products):
        inner = [dot(x, wide[256:512]) for x in products]
        twisted = []
        for x in inner:
            re, im = x[:, :128], x[:, 128:]
            c, s = cos[...], sin[...]
            twisted.append(
                jnp.concatenate([re * c - im * s, re * s + im * c], axis=0).astype(BF16)
            )
        for w, x in zip(ws, twisted):
            xt[w] = dot(wide[1024:1152], x).astype(BF16)

    def product(x, y):
        xr, xi, yr, yi = x[:, :128], x[:, 128:], y[:, :128], y[:, 128:]
        return jnp.concatenate([xr * yr - xi * yi, xr * yi + xi * yr], axis=1).astype(BF16)

    def conj_product(x, y):
        xr, xi, yr, yi = x[:, :128], x[:, 128:], y[:, :128], y[:, 128:]
        return jnp.concatenate([xr * yr + xi * yi, xr * yi - xi * yr], axis=1).astype(BF16)

    def groups(body):
        @pl.loop(0, W // GROUP)
        def _(i):
            body([i * GROUP + j for j in range(GROUP)])

    swap_blocks(taps_block, xt_store)

    def taps_step(ws):
        for w, x in zip(ws, forward(ws)):
            spec_h[w] = x.astype(BF16)

    groups(taps_step)

    wait_recv(0)
    swap_blocks(recv_block(0), xt_store)

    def gated_step(ws):
        found = forward(ws)
        for w, x in zip(ws, found):
            spec_g[w] = x.astype(BF16)
        backward(ws, [product(x, spec_h[w].astype(F32)) for w, x in zip(ws, found)])

    groups(gated_step)
    swap_blocks(xt_block, send_store(2))
    start_sends(2)

    wait_recv(1)
    swap_blocks(recv_block(1), xt_store)

    def grad_step(ws):
        found = forward(ws)
        for w, x in zip(ws, found):
            spec_q[w] = x.astype(BF16)
        backward(ws, [conj_product(spec_h[w].astype(F32), x) for w, x in zip(ws, found)])

    groups(grad_step)
    swap_blocks(xt_block, send_store(3))
    start_sends(3)

    def filter_step(ws):
        backward(ws, [conj_product(spec_g[w].astype(F32), spec_q[w].astype(F32)) for w in ws])

    groups(filter_step)
    swap_blocks(xt_block, fg_store)

    def turned(slot, i):
        rows = recv[slot, pl.ds(pl.multiple_of(i * 8, 8), 8)].reshape(256, 128)
        return dot_nt(wide[512:640, 0:128], rows)

    def gate_out(slot, pairs):
        @pl.loop(0, C // 256 // UNROLL)
        def _(i):
            found = [turned(slot, i * UNROLL + u) for u in range(UNROLL)]
            for u in range(UNROLL):
                cols = pl.ds(pl.multiple_of(i * (256 * UNROLL) + u * 256, 256), 256)
                for out_ref, gate in pairs:
                    out_ref[:, cols] = (gate[:, cols].astype(F32) * found[u]).astype(BF16)

    wait_recv(2)
    gate_out(2, [(qg_ref, g)])
    wait_recv(3)
    gate_out(3, [(kg_ref, v), (vg_ref, k)])

    for slot in range(4):
        wait_send(slot)


def place(*refs):
    *pairs, sem = refs
    half = len(pairs) // 2
    copies = [
        pltpu.make_async_copy(src, dst, sem.at[i])
        for i, (src, dst) in enumerate(zip(pairs[:half], pairs[half:]))
    ]
    for copy in copies:
        copy.start()
    for copy in copies:
        copy.wait()


def local(queries, keys, values, grad_out, filter_param):
    wide, first, twist = make_tables()
    operands = (queries, keys, values, grad_out, filter_param.T, wide, first, twist)
    hbm = pl.BlockSpec(memory_space=pltpu.HBM)
    vmem = pl.BlockSpec(memory_space=pltpu.VMEM)
    rows = (N, C)
    out = pl.pallas_call(
        kernel,
        out_shape=[pltpu.VMEM(rows, BF16)] * 3
        + [pltpu.VMEM((W, N * N), F32)],
        in_specs=[hbm] * 8,
        out_specs=[vmem] * 4,
        scratch_shapes=[
            pltpu.VMEM(rows, BF16),
            pltpu.VMEM(rows, BF16),
            pltpu.VMEM(rows, BF16),
            pltpu.VMEM(rows, BF16),
            pltpu.VMEM((W, N * N), F32),
            pltpu.VMEM(wide.shape, BF16),
            pltpu.VMEM(first.shape, BF16),
            pltpu.VMEM(twist.shape, F32),
            pltpu.VMEM((4, N, W, 128), BF16),
            pltpu.VMEM((4, N, W, 128), BF16),
            pltpu.VMEM((W, 128, 128), BF16),
            pltpu.VMEM((W, 128, 256), BF16),
            pltpu.VMEM((W, 128, 256), BF16),
            pltpu.VMEM((W, 128, 256), BF16),
            pltpu.SemaphoreType.DMA((8,)),
            pltpu.SemaphoreType.DMA((4,)),
            pltpu.SemaphoreType.DMA((4,)),
            pltpu.SemaphoreType.DMA((4,)),
        ],
        compiler_params=pltpu.CompilerParams(
            collective_id=0, has_side_effects=True, vmem_limit_bytes=40 << 20
        ),
        cost_estimate=pl.CostEstimate(flops=5 << 30, bytes_accessed=11 << 20, transcendentals=0),
    )(*[pltpu.with_memory_space_constraint(x, pltpu.HBM) for x in operands])
    query_grad, key_grad, value_grad, filter_grad = pl.pallas_call(
        place,
        out_shape=[jax.ShapeDtypeStruct(x.shape, x.dtype) for x in out],
        in_specs=[pl.BlockSpec(memory_space=pl.ANY)] * 4,
        out_specs=[hbm] * 4,
        scratch_shapes=[pltpu.SemaphoreType.DMA((4,))],
        compiler_params=pltpu.CompilerParams(vmem_limit_bytes=1 << 20),
    )(*out)
    return query_grad, key_grad, value_grad, filter_grad.T


def solution(mesh):
    split = P(("dp", "ctx"), None)
    channels = P(None, ("dp", "ctx"))
    return jax.shard_map(
        local,
        mesh=mesh,
        in_specs=(split, split, split, split, channels),
        out_specs=(split, split, split, channels),
        check_vma=False,
    )
```

```python
import functools
import math

import jax
import jax.numpy as jnp
import numpy as np
from jax import lax
from jax.experimental import pallas as pl
from jax.experimental.pallas import tpu as pltpu
from jax.sharding import PartitionSpec as P

MESH = pl.DeviceIdType.MESH
F32 = jnp.float32
BF16 = jnp.bfloat16
N = 128
W = 32
HALF = W // 2
C = N * W
GROUP = 4
UNROLL = 4
SWAP_UNROLL = 4


def make_tables():
    a = np.arange(128, dtype=np.float64)
    k = np.arange(128, dtype=np.float64)
    outer = 2.0 * np.pi * np.outer(k + 0.5, a) / 256.0
    first = np.concatenate([np.cos(outer), -np.sin(outer)], axis=0)
    last = first.T * (2.0 / 32768.0 / 128.0)
    inner = 2.0 * np.pi * (np.outer(a, a) % 128) / 128.0
    c, s = np.cos(inner), np.sin(inner)
    second = np.block([[c, -s], [s, c]])
    twist = 2.0 * np.pi * np.outer(k + 0.5, a) / 32768.0
    index = np.arange(256)
    swap = np.zeros((256, 256))
    swap[index, (index % 16) * 16 + index // 16] = 1.0
    wide = np.concatenate([second, second.T, np.eye(256), swap, last], axis=0)
    return (
        jnp.asarray(wide.astype(np.float32), BF16),
        jnp.asarray(first.astype(np.float32), BF16),
        jnp.asarray(np.concatenate([np.cos(twist), np.sin(twist)], axis=0), F32),
    )


def dot(x, y):
    return lax.dot_general(x, y, (((1,), (0,)), ((), ())), preferred_element_type=F32)


def dot_nt(x, y):
    return lax.dot_general(x, y, (((1,), (1,)), ((), ())), preferred_element_type=F32)


def kernel(
    q_hbm, k_hbm, v_hbm, g_hbm, taps_hbm, wide_hbm, first_hbm, twist_hbm,
    qg_ref, kg_ref, vg_ref, fg_ref,
    q, k, v, g, taps, wide, first, twist,
    send, recv, xt, spec_h, spec_g, spec_q,
    load_sem, send_sem, recv_sem, own_sem,
):
    dp, ctx = lax.axis_index("dp"), lax.axis_index("ctx")
    me = dp * 16 + ctx
    cx, cy, cz, cc = (dp % 2) * 2 + (ctx // 2) % 2, ctx // 4, dp // 2, ctx % 2

    loads = [
        pltpu.make_async_copy(src, dst, load_sem.at[i])
        for i, (src, dst) in enumerate(
            [(wide_hbm, wide), (k_hbm, k), (v_hbm, v), (q_hbm, q), (g_hbm, g),
             (first_hbm, first), (twist_hbm, twist), (taps_hbm, taps)]
        )
    ]
    for load in loads:
        load.start()

    xs = [(cx + r) % 4 for r in range(4)]
    x_dp = [x // 2 for x in xs]
    x_ctx = [(x % 2) * 2 for x in xs]
    y_ctx = [((cy + r) % 4) * 4 for r in range(4)]
    c_ctx = [cc, 1 - cc]

    def partners(visit):
        @pl.loop(0, 8)
        def _(m):
            z_dp = [((cz + m + r) % 4) * 2 for r in range(4)]
            far = m // 4
            c_now = [far + (1 - 2 * far) * c for c in c_ctx]
            for n in range(4):
                for r in range(4):
                    d = z_dp[(n + r) % 4] + x_dp[r]
                    e = y_ctx[(n + r) % 4] + x_ctx[r] + c_now[r % 2]
                    if n + r == 0:
                        pl.when(m > 0)(functools.partial(visit, d, e))
                    else:
                        visit(d, e)

    barrier = pltpu.get_barrier_semaphore()

    partners(
        lambda d, e: pl.semaphore_signal(barrier, inc=1, device_id=(d, e), device_id_type=MESH)
    )

    ident = wide.at[512:768]
    swap = wide.at[768:1024]

    def gate_in(left, right, slot):
        @pl.loop(0, C // 256 // UNROLL)
        def _(i):
            turned = []
            for u in range(UNROLL):
                cols = pl.ds(pl.multiple_of(i * (256 * UNROLL) + u * 256, 256), 256)
                gated = (left[:, cols].astype(F32) * right[:, cols].astype(F32)).astype(BF16)
                turned.append(dot_nt(ident[...], gated).astype(BF16))
            for u in range(UNROLL):
                block = turned[u].reshape(8, W, 128)
                rows = pl.ds(pl.multiple_of(i * (8 * UNROLL) + u * 8, 8), 8)
                send[slot, rows] = block[:, :HALF]
                send[slot + 1, rows] = block[:, HALF:]

    for load in loads[:3]:
        load.wait()
    gate_in(k, v, 0)
    pl.semaphore_wait(barrier, N - 1)

    def start_sends(slot):

        def visit(d, e):
            pltpu.make_async_remote_copy(
                src_ref=send.at[slot, d * 16 + e],
                dst_ref=recv.at[slot, me],
                send_sem=send_sem.at[slot],
                recv_sem=recv_sem.at[slot],
                device_id=(d, e),
                device_id_type=MESH,
            ).start()

        partners(visit)
        pltpu.make_async_copy(send.at[slot, me], recv.at[slot, me], own_sem.at[slot]).start()

    def wait_recv(slot):

        others = recv.at[slot, pl.ds(0, N - 1)]
        pltpu.make_async_copy(others, others, recv_sem.at[slot]).wait()
        pltpu.make_async_copy(send.at[slot, me], recv.at[slot, me], own_sem.at[slot]).wait()

    def wait_send(slot):

        others = send.at[slot, pl.ds(0, N - 1)]
        pltpu.make_async_copy(others, others, send_sem.at[slot]).wait()

    start_sends(0)
    start_sends(1)
    for load in loads[3:5]:
        load.wait()
    gate_in(g, q, 2)
    start_sends(2)
    start_sends(3)
    for load in loads[5:]:
        load.wait()

    cos, sin = twist.at[0:128], twist.at[128:256]

    def swap_blocks(half, load_block, store_block):
        @pl.loop(0, 8 // SWAP_UNROLL)
        def _(i):
            blocks = [i * SWAP_UNROLL + u for u in range(SWAP_UNROLL)]
            found = [dot(swap[...], load_block(half, block)) for block in blocks]
            for block, x in zip(blocks, found):
                store_block(half, block, x)

    def sixteen(i):
        return pl.ds(pl.multiple_of(i * 16, 16), 16)

    def half_of(half):
        return pl.ds(half * HALF, HALF)

    def recv_block(slot):
        return lambda half, i: recv[slot + half, sixteen(i)].reshape(256, 128)

    def taps_block(half, i):
        parts = []
        for s in range(16):
            lanes = pl.ds(pl.multiple_of((i * 16 + s) * 128, 128), 128)
            parts.append(taps[half_of(half), lanes])
        return jnp.concatenate(parts, axis=0).astype(BF16)

    def xt_store(half, i, block):
        xt[half_of(half), sixteen(i), :] = block.astype(BF16).reshape(16, 16, 128)

    def xt_block(half, i):
        return xt[half_of(half), sixteen(i), :].reshape(256, 128)

    def send_store(slot):
        def store(half, i, block):
            send[slot + half, sixteen(i)] = block.astype(BF16).reshape(16, 16, 128)

        return store

    def fg_store(half, i, block):
        for s in range(16):
            lanes = pl.ds(pl.multiple_of((i * 16 + s) * 128, 128), 128)
            fg_ref[half_of(half), lanes] = block[s * 16 : (s + 1) * 16]

    def forward(ws):
        outer = [dot(first[...], xt[w]) for w in ws]
        twisted = []
        for x in outer:
            re, im = x[:128], x[128:]
            c, s = cos[...], sin[...]
            twisted.append(
                jnp.concatenate([re * c + im * s, im * c - re * s], axis=1).astype(BF16)
            )
        return [dot(x, wide[0:256]) for x in twisted]

    def backward(ws, products):
        inner = [dot(x, wide[256:512]) for x in products]
        twisted = []
        for x in inner:
            re, im = x[:, :128], x[:, 128:]
            c, s = cos[...], sin[...]
            twisted.append(
                jnp.concatenate([re * c - im * s, re * s + im * c], axis=0).astype(BF16)
            )
        for w, x in zip(ws, twisted):
            xt[w] = dot(wide[1024:1152], x).astype(BF16)

    def product(x, y):
        xr, xi, yr, yi = x[:, :128], x[:, 128:], y[:, :128], y[:, 128:]
        return jnp.concatenate([xr * yr - xi * yi, xr * yi + xi * yr], axis=1).astype(BF16)

    def conj_product(x, y):
        xr, xi, yr, yi = x[:, :128], x[:, 128:], y[:, :128], y[:, 128:]
        return jnp.concatenate([xr * yr + xi * yi, xr * yi - xi * yr], axis=1).astype(BF16)

    def groups(half, body):
        @pl.loop(half * HALF // GROUP, (half + 1) * HALF // GROUP)
        def _(i):
            body([i * GROUP + j for j in range(GROUP)])

    def taps_step(ws):
        for w, x in zip(ws, forward(ws)):
            spec_h[w] = x.astype(BF16)

    def gated_step(ws):
        found = forward(ws)
        for w, x in zip(ws, found):
            spec_g[w] = x.astype(BF16)
        backward(ws, [product(x, spec_h[w].astype(F32)) for w, x in zip(ws, found)])

    def grad_step(ws):
        found = forward(ws)
        for w, x in zip(ws, found):
            spec_q[w] = x.astype(BF16)
        backward(ws, [conj_product(spec_h[w].astype(F32), x) for w, x in zip(ws, found)])

    def filter_step(ws):
        backward(ws, [conj_product(spec_g[w].astype(F32), spec_q[w].astype(F32)) for w in ws])

    for half in range(2):
        swap_blocks(half, taps_block, xt_store)
        groups(half, taps_step)
    for slot, step in ((0, gated_step), (2, grad_step)):
        for half in range(2):
            wait_recv(slot + half)
            swap_blocks(half, recv_block(slot), xt_store)
            groups(half, step)
            swap_blocks(half, xt_block, send_store(slot + 4))
            start_sends(slot + 4 + half)
    for half in range(2):
        groups(half, filter_step)
        swap_blocks(half, xt_block, fg_store)

    def turned(slot, i):
        rows = pl.ds(pl.multiple_of(i * 8, 8), 8)
        both = jnp.concatenate([recv[slot, rows], recv[slot + 1, rows]], axis=1)
        return dot_nt(wide[512:640, 0:128], both.reshape(256, 128))

    def gate_out(slot, pairs):
        @pl.loop(0, C // 256 // UNROLL)
        def _(i):
            found = [turned(slot, i * UNROLL + u) for u in range(UNROLL)]
            for u in range(UNROLL):
                cols = pl.ds(pl.multiple_of(i * (256 * UNROLL) + u * 256, 256), 256)
                for out_ref, gate in pairs:
                    out_ref[:, cols] = (gate[:, cols].astype(F32) * found[u]).astype(BF16)

    wait_recv(4)
    wait_recv(5)
    gate_out(4, [(qg_ref, g)])
    wait_recv(6)
    wait_recv(7)
    gate_out(6, [(kg_ref, v), (vg_ref, k)])
    for slot in range(8):
        wait_send(slot)


def place(*refs):
    *pairs, sem = refs
    half = len(pairs) // 2
    copies = [
        pltpu.make_async_copy(src, dst, sem.at[i])
        for i, (src, dst) in enumerate(zip(pairs[:half], pairs[half:]))
    ]
    for copy in copies:
        copy.start()
    for copy in copies:
        copy.wait()


def local(queries, keys, values, grad_out, filter_param):
    wide, first, twist = make_tables()
    operands = (queries, keys, values, grad_out, filter_param.T, wide, first, twist)
    hbm = pl.BlockSpec(memory_space=pltpu.HBM)
    vmem = pl.BlockSpec(memory_space=pltpu.VMEM)
    rows = (N, C)
    out = pl.pallas_call(
        kernel,
        out_shape=[pltpu.VMEM(rows, BF16)] * 3
        + [pltpu.VMEM((W, N * N), F32)],
        in_specs=[hbm] * 8,
        out_specs=[vmem] * 4,
        scratch_shapes=[
            pltpu.VMEM(rows, BF16),
            pltpu.VMEM(rows, BF16),
            pltpu.VMEM(rows, BF16),
            pltpu.VMEM(rows, BF16),
            pltpu.VMEM((W, N * N), F32),
            pltpu.VMEM(wide.shape, BF16),
            pltpu.VMEM(first.shape, BF16),
            pltpu.VMEM(twist.shape, F32),
            pltpu.VMEM((8, N, HALF, 128), BF16),
            pltpu.VMEM((8, N, HALF, 128), BF16),
            pltpu.VMEM((W, 128, 128), BF16),
            pltpu.VMEM((W, 128, 256), BF16),
            pltpu.VMEM((W, 128, 256), BF16),
            pltpu.VMEM((W, 128, 256), BF16),
            pltpu.SemaphoreType.DMA((8,)),
            pltpu.SemaphoreType.DMA((8,)),
            pltpu.SemaphoreType.DMA((8,)),
            pltpu.SemaphoreType.DMA((8,)),
        ],
        compiler_params=pltpu.CompilerParams(
            collective_id=0, has_side_effects=True, vmem_limit_bytes=40 << 20
        ),
        cost_estimate=pl.CostEstimate(flops=5 << 30, bytes_accessed=11 << 20, transcendentals=0),
    )(*[pltpu.with_memory_space_constraint(x, pltpu.HBM) for x in operands])
    query_grad, key_grad, value_grad, filter_grad = pl.pallas_call(
        place,
        out_shape=[jax.ShapeDtypeStruct(x.shape, x.dtype) for x in out],
        in_specs=[pl.BlockSpec(memory_space=pl.ANY)] * 4,
        out_specs=[hbm] * 4,
        scratch_shapes=[pltpu.SemaphoreType.DMA((4,))],
        compiler_params=pltpu.CompilerParams(vmem_limit_bytes=1 << 20),
    )(*out)
    return query_grad, key_grad, value_grad, filter_grad.T


def solution(mesh):
    split = P(("dp", "ctx"), None)
    channels = P(None, ("dp", "ctx"))
    return jax.shard_map(
        local,
        mesh=mesh,
        in_specs=(split, split, split, split, channels),
        out_specs=(split, split, split, channels),
        check_vma=False,
    )
```

```python
import functools
import math

import jax
import jax.numpy as jnp
import numpy as np
from jax import lax
from jax.experimental import pallas as pl
from jax.experimental.pallas import tpu as pltpu
from jax.sharding import PartitionSpec as P

MESH = pl.DeviceIdType.MESH
F32 = jnp.float32
BF16 = jnp.bfloat16
N = 128
W = 32
HALF = W // 2
C = N * W
GROUP = 4
UNROLL = 4
SWAP_UNROLL = 4


def make_tables():
    a = np.arange(128, dtype=np.float64)
    k = np.arange(128, dtype=np.float64)
    outer = 2.0 * np.pi * np.outer(k + 0.5, a) / 256.0
    first = np.concatenate([np.cos(outer), -np.sin(outer)], axis=0)
    last = first.T * (2.0 / 32768.0 / 128.0)
    inner = 2.0 * np.pi * (np.outer(a, a) % 128) / 128.0
    c, s = np.cos(inner), np.sin(inner)
    second = np.block([[c, -s], [s, c]])
    twist = 2.0 * np.pi * np.outer(k + 0.5, a) / 32768.0
    index = np.arange(256)
    swap = np.zeros((256, 256))
    swap[index, (index % 16) * 16 + index // 16] = 1.0
    wide = np.concatenate([second, second.T, np.eye(256), swap, last], axis=0)
    return (
        jnp.asarray(wide.astype(np.float32), BF16),
        jnp.asarray(first.astype(np.float32), BF16),
        jnp.asarray(np.concatenate([np.cos(twist), np.sin(twist)], axis=0), F32),
    )


def dot(x, y):
    return lax.dot_general(x, y, (((1,), (0,)), ((), ())), preferred_element_type=F32)


def dot_nt(x, y):
    return lax.dot_general(x, y, (((1,), (1,)), ((), ())), preferred_element_type=F32)


def gate_out(i, unit, low, high, pairs):
    found = []
    for u in range(UNROLL):
        rows = pl.ds(pl.multiple_of((i * UNROLL + u) * 8, 8), 8)
        both = jnp.concatenate([low[rows], high[rows]], axis=1)
        found.append(dot_nt(unit, both.reshape(256, 128)))
    for u in range(UNROLL):
        cols = pl.ds(pl.multiple_of((i * UNROLL + u) * 256, 256), 256)
        for out_ref, gate in pairs:
            out_ref[:, cols] = (gate[:, cols].astype(F32) * found[u]).astype(BF16)


def kernel(
    q_hbm, k_hbm, v_hbm, g_hbm, taps_hbm, wide_hbm, first_hbm, twist_hbm,
    qg_ref, fg_ref, back, k, v,
    q, g, taps, wide, first, twist,
    send, recv, xt, spec_h, spec_g, spec_q,
    load_sem, send_sem, recv_sem, own_sem,
):
    dp, ctx = lax.axis_index("dp"), lax.axis_index("ctx")
    me = dp * 16 + ctx
    cx, cy, cz, cc = (dp % 2) * 2 + (ctx // 2) % 2, ctx // 4, dp // 2, ctx % 2

    loads = [
        pltpu.make_async_copy(src, dst, load_sem.at[i])
        for i, (src, dst) in enumerate(
            [(wide_hbm, wide), (k_hbm, k), (v_hbm, v), (q_hbm, q), (g_hbm, g),
             (first_hbm, first), (twist_hbm, twist), (taps_hbm, taps)]
        )
    ]
    for load in loads[:3]:
        load.start()

    xs = [(cx + r) % 4 for r in range(4)]
    x_dp = [x // 2 for x in xs]
    x_ctx = [(x % 2) * 2 for x in xs]
    y_ctx = [((cy + r) % 4) * 4 for r in range(4)]
    c_ctx = [cc, 1 - cc]

    def partners(visit):
        @pl.loop(0, 8)
        def _(m):
            z_dp = [((cz + m + r) % 4) * 2 for r in range(4)]
            far = m // 4
            c_now = [far + (1 - 2 * far) * c for c in c_ctx]
            for n in range(4):
                for r in range(4):
                    d = z_dp[(n + r) % 4] + x_dp[r]
                    e = y_ctx[(n + r) % 4] + x_ctx[r] + c_now[r % 2]
                    if n + r == 0:
                        pl.when(m > 0)(functools.partial(visit, d, e))
                    else:
                        visit(d, e)

    barrier = pltpu.get_barrier_semaphore()

    partners(
        lambda d, e: pl.semaphore_signal(barrier, inc=1, device_id=(d, e), device_id_type=MESH)
    )
    for load in loads[3:]:
        load.start()

    ident = wide.at[512:768]
    swap = wide.at[768:1024]

    def gate_in(left, right, slot):
        @pl.loop(0, C // 256 // UNROLL)
        def _(i):
            turned = []
            for u in range(UNROLL):
                cols = pl.ds(pl.multiple_of(i * (256 * UNROLL) + u * 256, 256), 256)
                gated = (left[:, cols].astype(F32) * right[:, cols].astype(F32)).astype(BF16)
                turned.append(dot_nt(ident[...], gated).astype(BF16))
            for u in range(UNROLL):
                block = turned[u].reshape(8, W, 128)
                rows = pl.ds(pl.multiple_of(i * (8 * UNROLL) + u * 8, 8), 8)
                send[slot, rows] = block[:, :HALF]
                send[slot + 1, rows] = block[:, HALF:]

    for load in loads[:3]:
        load.wait()
    gate_in(k, v, 0)
    pl.semaphore_wait(barrier, N - 1)

    def landing(slot):
        return recv.at[slot] if slot < 6 else back.at[slot - 6]

    def start_sends(slot):

        def visit(d, e):
            pltpu.make_async_remote_copy(
                src_ref=send.at[slot, d * 16 + e],
                dst_ref=landing(slot).at[me],
                send_sem=send_sem.at[slot],
                recv_sem=recv_sem.at[slot],
                device_id=(d, e),
                device_id_type=MESH,
            ).start()

        partners(visit)
        pltpu.make_async_copy(send.at[slot, me], landing(slot).at[me], own_sem.at[slot]).start()

    def wait_recv(slot):

        others = landing(slot).at[pl.ds(0, N - 1)]
        pltpu.make_async_copy(others, others, recv_sem.at[slot]).wait()
        pltpu.make_async_copy(send.at[slot, me], landing(slot).at[me], own_sem.at[slot]).wait()

    def wait_send(slot):

        others = send.at[slot, pl.ds(0, N - 1)]
        pltpu.make_async_copy(others, others, send_sem.at[slot]).wait()

    start_sends(0)
    start_sends(1)
    for load in loads[3:5]:
        load.wait()
    gate_in(g, q, 2)
    start_sends(2)
    start_sends(3)
    for load in loads[5:]:
        load.wait()

    cos, sin = twist.at[0:128], twist.at[128:256]

    def swap_blocks(half, load_block, store_block):
        @pl.loop(0, 8 // SWAP_UNROLL)
        def _(i):
            blocks = [i * SWAP_UNROLL + u for u in range(SWAP_UNROLL)]
            found = [dot(swap[...], load_block(half, block)) for block in blocks]
            for block, x in zip(blocks, found):
                store_block(half, block, x)

    def sixteen(i):
        return pl.ds(pl.multiple_of(i * 16, 16), 16)

    def half_of(half):
        return pl.ds(half * HALF, HALF)

    def recv_block(slot):
        return lambda half, i: recv[slot + half, sixteen(i)].reshape(256, 128)

    def taps_block(half, i):
        parts = []
        for s in range(16):
            lanes = pl.ds(pl.multiple_of((i * 16 + s) * 128, 128), 128)
            parts.append(taps[half_of(half), lanes])
        return jnp.concatenate(parts, axis=0).astype(BF16)

    def xt_store(half, i, block):
        xt[half_of(half), sixteen(i), :] = block.astype(BF16).reshape(16, 16, 128)

    def xt_block(half, i):
        return xt[half_of(half), sixteen(i), :].reshape(256, 128)

    def send_store(slot):
        def store(half, i, block):
            send[slot + half, sixteen(i)] = block.astype(BF16).reshape(16, 16, 128)

        return store

    def fg_store(half, i, block):
        for s in range(16):
            lanes = pl.ds(pl.multiple_of((i * 16 + s) * 128, 128), 128)
            fg_ref[half_of(half), lanes] = block[s * 16 : (s + 1) * 16]

    def forward(ws):
        outer = [dot(first[...], xt[w]) for w in ws]
        twisted = []
        for x in outer:
            re, im = x[:128], x[128:]
            c, s = cos[...], sin[...]
            twisted.append(
                jnp.concatenate([re * c + im * s, im * c - re * s], axis=1).astype(BF16)
            )
        return [dot(x, wide[0:256]) for x in twisted]

    def backward(ws, products):
        inner = [dot(x, wide[256:512]) for x in products]
        twisted = []
        for x in inner:
            re, im = x[:, :128], x[:, 128:]
            c, s = cos[...], sin[...]
            twisted.append(
                jnp.concatenate([re * c - im * s, re * s + im * c], axis=0).astype(BF16)
            )
        for w, x in zip(ws, twisted):
            xt[w] = dot(wide[1024:1152], x).astype(BF16)

    def product(x, y):
        xr, xi, yr, yi = x[:, :128], x[:, 128:], y[:, :128], y[:, 128:]
        return jnp.concatenate([xr * yr - xi * yi, xr * yi + xi * yr], axis=1).astype(BF16)

    def conj_product(x, y):
        xr, xi, yr, yi = x[:, :128], x[:, 128:], y[:, :128], y[:, 128:]
        return jnp.concatenate([xr * yr + xi * yi, xr * yi - xi * yr], axis=1).astype(BF16)

    def groups(half, body):
        @pl.loop(half * HALF // GROUP, (half + 1) * HALF // GROUP)
        def _(i):
            body([i * GROUP + j for j in range(GROUP)])

    def taps_step(ws):
        for w, x in zip(ws, forward(ws)):
            spec_h[w] = x.astype(BF16)

    def gated_step(ws):
        found = forward(ws)
        for w, x in zip(ws, found):
            spec_g[w] = x.astype(BF16)
        backward(ws, [product(x, spec_h[w].astype(F32)) for w, x in zip(ws, found)])

    def grad_step(ws):
        found = forward(ws)
        for w, x in zip(ws, found):
            spec_q[w] = x.astype(BF16)
        backward(ws, [conj_product(spec_h[w].astype(F32), x) for w, x in zip(ws, found)])

    def filter_step(ws):
        backward(ws, [conj_product(spec_g[w].astype(F32), spec_q[w].astype(F32)) for w in ws])

    for half in range(2):
        swap_blocks(half, taps_block, xt_store)
        groups(half, taps_step)
    for slot, step in ((0, gated_step), (2, grad_step)):
        for half in range(2):
            wait_recv(slot + half)
            swap_blocks(half, recv_block(slot), xt_store)
            groups(half, step)
            swap_blocks(half, xt_block, send_store(slot + 4))
            start_sends(slot + 4 + half)
    for half in range(2):
        groups(half, filter_step)
        swap_blocks(half, xt_block, fg_store)

    wait_recv(4)
    wait_recv(5)

    @pl.loop(0, C // 256 // UNROLL)
    def _(i):
        gate_out(i, wide[512:640, 0:128], recv.at[4], recv.at[5], [(qg_ref, g)])

    wait_recv(6)
    wait_recv(7)
    for slot in range(8):
        wait_send(slot)


def finish(
    qg, fg, back, k, v, qg_hbm, fg_hbm, kg_hbm, vg_hbm, kg, vg, sem
):
    copies = [
        pltpu.make_async_copy(fg, fg_hbm, sem.at[0]),
        pltpu.make_async_copy(qg, qg_hbm, sem.at[1]),
    ]
    for copy in copies:
        copy.start()
    rows = lax.broadcasted_iota(jnp.int32, (128, 128), 0)
    unit = (rows == lax.broadcasted_iota(jnp.int32, (128, 128), 1)).astype(F32).astype(BF16)
    steps = C // 256 // UNROLL
    for i in range(steps):
        gate_out(i, unit, back.at[0], back.at[1], [(kg, v), (vg, k)])
        cols = pl.ds(i * 256 * UNROLL, 256 * UNROLL)
        for j, (src, dst) in enumerate([(kg, kg_hbm), (vg, vg_hbm)]):
            copy = pltpu.make_async_copy(src.at[:, cols], dst.at[:, cols], sem.at[2 + 2 * i + j])
            copy.start()
            copies.append(copy)
    for copy in copies:
        copy.wait()


def local(queries, keys, values, grad_out, filter_param):
    wide, first, twist = make_tables()
    operands = (queries, keys, values, grad_out, filter_param.T, wide, first, twist)
    hbm = pl.BlockSpec(memory_space=pltpu.HBM)
    vmem = pl.BlockSpec(memory_space=pltpu.VMEM)
    rows = (N, C)
    out = pl.pallas_call(
        kernel,
        out_shape=[
            pltpu.VMEM(rows, BF16),
            pltpu.VMEM((W, N * N), F32),
            pltpu.VMEM((2, N, HALF, 128), BF16),
            pltpu.VMEM(rows, BF16),
            pltpu.VMEM(rows, BF16),
        ],
        in_specs=[hbm] * 8,
        out_specs=[vmem] * 5,
        scratch_shapes=[
            pltpu.VMEM(rows, BF16),
            pltpu.VMEM(rows, BF16),
            pltpu.VMEM((W, N * N), F32),
            pltpu.VMEM(wide.shape, BF16),
            pltpu.VMEM(first.shape, BF16),
            pltpu.VMEM(twist.shape, F32),
            pltpu.VMEM((8, N, HALF, 128), BF16),
            pltpu.VMEM((6, N, HALF, 128), BF16),
            pltpu.VMEM((W, 128, 128), BF16),
            pltpu.VMEM((W, 128, 256), BF16),
            pltpu.VMEM((W, 128, 256), BF16),
            pltpu.VMEM((W, 128, 256), BF16),
            pltpu.SemaphoreType.DMA((8,)),
            pltpu.SemaphoreType.DMA((8,)),
            pltpu.SemaphoreType.DMA((8,)),
            pltpu.SemaphoreType.DMA((8,)),
        ],
        compiler_params=pltpu.CompilerParams(
            collective_id=0, has_side_effects=True, vmem_limit_bytes=40 << 20
        ),
        cost_estimate=pl.CostEstimate(flops=5 << 30, bytes_accessed=11 << 20, transcendentals=0),
    )(*[pltpu.with_memory_space_constraint(x, pltpu.HBM) for x in operands])
    query_grad, filter_grad, key_grad, value_grad = pl.pallas_call(
        finish,
        out_shape=[
            jax.ShapeDtypeStruct(rows, BF16),
            jax.ShapeDtypeStruct((W, N * N), F32),
            jax.ShapeDtypeStruct(rows, BF16),
            jax.ShapeDtypeStruct(rows, BF16),
        ],
        in_specs=[pl.BlockSpec(memory_space=pl.ANY)] * 2 + [vmem] * 3,
        out_specs=[hbm] * 4,
        scratch_shapes=[
            pltpu.VMEM(rows, BF16),
            pltpu.VMEM(rows, BF16),
            pltpu.SemaphoreType.DMA((2 + 2 * (C // 256 // UNROLL),)),
        ],
        compiler_params=pltpu.CompilerParams(vmem_limit_bytes=8 << 20),
    )(*out)
    return query_grad, key_grad, value_grad, filter_grad.T


def solution(mesh):
    split = P(("dp", "ctx"), None)
    channels = P(None, ("dp", "ctx"))
    return jax.shard_map(
        local,
        mesh=mesh,
        in_specs=(split, split, split, split, channels),
        out_specs=(split, split, split, channels),
        check_vma=False,
    )
```

```python
import functools
import math

import jax
import jax.numpy as jnp
import numpy as np
from jax import lax
from jax.experimental import pallas as pl
from jax.experimental.pallas import tpu as pltpu
from jax.sharding import PartitionSpec as P

MESH = pl.DeviceIdType.MESH
F32 = jnp.float32
BF16 = jnp.bfloat16
N = 128
W = 32
HALF = W // 2
C = N * W
GROUP = 4
UNROLL = 4
SWAP_UNROLL = 4


def make_tables():
    a = np.arange(128, dtype=np.float64)
    k = np.arange(128, dtype=np.float64)
    outer = 2.0 * np.pi * np.outer(k + 0.5, a) / 256.0
    first = np.concatenate([np.cos(outer), -np.sin(outer)], axis=0)
    last = first.T * (2.0 / 32768.0 / 128.0)
    inner = 2.0 * np.pi * (np.outer(a, a) % 128) / 128.0
    c, s = np.cos(inner), np.sin(inner)
    second = np.block([[c, -s], [s, c]])
    twist = 2.0 * np.pi * np.outer(k + 0.5, a) / 32768.0
    index = np.arange(256)
    swap = np.zeros((256, 256))
    swap[index, (index % 16) * 16 + index // 16] = 1.0
    first_high = first.astype(BF16).astype(np.float64)
    first = np.concatenate([first_high, first - first_high], axis=1)
    wide = np.concatenate([second, second.T, np.eye(256), swap, last], axis=0)
    return (
        jnp.asarray(wide.astype(np.float32), BF16),
        jnp.asarray(first.astype(np.float32), BF16),
        jnp.asarray(np.concatenate([np.cos(twist), np.sin(twist)], axis=0), F32),
    )


def dot(x, y):
    return lax.dot_general(x, y, (((1,), (0,)), ((), ())), preferred_element_type=F32)


def dot_nt(x, y):
    return lax.dot_general(x, y, (((1,), (1,)), ((), ())), preferred_element_type=F32)


def gate_out(i, unit, low, high, pairs):
    found = []
    for u in range(UNROLL):
        rows = pl.ds(pl.multiple_of((i * UNROLL + u) * 8, 8), 8)
        both = jnp.concatenate([low[rows], high[rows]], axis=1)
        found.append(dot_nt(unit, both.reshape(256, 128)))
    for u in range(UNROLL):
        cols = pl.ds(pl.multiple_of((i * UNROLL + u) * 256, 256), 256)
        for out_ref, gate in pairs:
            out_ref[:, cols] = (gate[:, cols].astype(F32) * found[u]).astype(BF16)


def kernel(
    q_hbm, k_hbm, v_hbm, g_hbm, taps_hbm, wide_hbm, first_hbm, twist_hbm,
    qg_ref, fg_ref, back, k, v,
    q, g, taps, wide, first, twist,
    send, recv, xt, xt_rest, spec_h, spec_g, spec_q,
    load_sem, send_sem, recv_sem, own_sem,
):
    dp, ctx = lax.axis_index("dp"), lax.axis_index("ctx")
    me = dp * 16 + ctx
    cx, cy, cz, cc = (dp % 2) * 2 + (ctx // 2) % 2, ctx // 4, dp // 2, ctx % 2

    loads = [
        pltpu.make_async_copy(src, dst, load_sem.at[i])
        for i, (src, dst) in enumerate(
            [(wide_hbm, wide), (k_hbm, k), (v_hbm, v), (q_hbm, q), (g_hbm, g),
             (first_hbm, first), (twist_hbm, twist), (taps_hbm, taps)]
        )
    ]
    for load in loads[:3]:
        load.start()

    xs = [(cx + r) % 4 for r in range(4)]
    x_dp = [x // 2 for x in xs]
    x_ctx = [(x % 2) * 2 for x in xs]
    y_ctx = [((cy + r) % 4) * 4 for r in range(4)]
    c_ctx = [cc, 1 - cc]

    def partners(visit):
        @pl.loop(0, 8)
        def _(m):
            z_dp = [((cz + m + r) % 4) * 2 for r in range(4)]
            far = m // 4
            c_now = [far + (1 - 2 * far) * c for c in c_ctx]
            for n in range(4):
                for r in range(4):
                    d = z_dp[(n + r) % 4] + x_dp[r]
                    e = y_ctx[(n + r) % 4] + x_ctx[r] + c_now[r % 2]
                    if n + r == 0:
                        pl.when(m > 0)(functools.partial(visit, d, e))
                    else:
                        visit(d, e)

    barrier = pltpu.get_barrier_semaphore()

    partners(
        lambda d, e: pl.semaphore_signal(barrier, inc=1, device_id=(d, e), device_id_type=MESH)
    )
    for load in loads[3:]:
        load.start()

    ident = wide.at[512:768]
    swap = wide.at[768:1024]

    def gate_in(left, right, slot):
        @pl.loop(0, C // 256 // UNROLL)
        def _(i):
            turned = []
            for u in range(UNROLL):
                cols = pl.ds(pl.multiple_of(i * (256 * UNROLL) + u * 256, 256), 256)
                gated = (left[:, cols].astype(F32) * right[:, cols].astype(F32)).astype(BF16)
                turned.append(dot_nt(ident[...], gated).astype(BF16))
            for u in range(UNROLL):
                block = turned[u].reshape(8, W, 128)
                rows = pl.ds(pl.multiple_of(i * (8 * UNROLL) + u * 8, 8), 8)
                send[slot, rows] = block[:, :HALF]
                send[slot + 1, rows] = block[:, HALF:]

    for load in loads[:3]:
        load.wait()
    gate_in(k, v, 0)
    pl.semaphore_wait(barrier, N - 1)

    def landing(slot):
        return recv.at[slot] if slot < 6 else back.at[slot - 6]

    def start_sends(slot):

        def visit(d, e):
            pltpu.make_async_remote_copy(
                src_ref=send.at[slot, d * 16 + e],
                dst_ref=landing(slot).at[me],
                send_sem=send_sem.at[slot],
                recv_sem=recv_sem.at[slot],
                device_id=(d, e),
                device_id_type=MESH,
            ).start()

        partners(visit)
        pltpu.make_async_copy(send.at[slot, me], landing(slot).at[me], own_sem.at[slot]).start()

    def wait_recv(slot):

        others = landing(slot).at[pl.ds(0, N - 1)]
        pltpu.make_async_copy(others, others, recv_sem.at[slot]).wait()
        pltpu.make_async_copy(send.at[slot, me], landing(slot).at[me], own_sem.at[slot]).wait()

    def wait_send(slot):

        others = send.at[slot, pl.ds(0, N - 1)]
        pltpu.make_async_copy(others, others, send_sem.at[slot]).wait()

    start_sends(0)
    start_sends(1)
    for load in loads[3:5]:
        load.wait()
    gate_in(g, q, 2)
    start_sends(2)
    start_sends(3)
    for load in loads[5:]:
        load.wait()

    cos, sin = twist.at[0:128], twist.at[128:256]

    def swap_blocks(half, load_block, store_block):
        @pl.loop(0, 8 // SWAP_UNROLL)
        def _(i):
            blocks = [i * SWAP_UNROLL + u for u in range(SWAP_UNROLL)]
            found = [dot(swap[...], load_block(half, block)) for block in blocks]
            for block, x in zip(blocks, found):
                store_block(half, block, x)

    def sixteen(i):
        return pl.ds(pl.multiple_of(i * 16, 16), 16)

    def half_of(half):
        return pl.ds(half * HALF, HALF)

    def recv_block(slot):
        return lambda half, i: recv[slot + half, sixteen(i)].reshape(256, 128)

    def taps_block(half, i):
        parts = []
        for s in range(16):
            lanes = pl.ds(pl.multiple_of((i * 16 + s) * 128, 128), 128)
            parts.append(taps[half_of(half), lanes])
        return jnp.concatenate(parts, axis=0).astype(BF16)

    def xt_store(half, i, block):
        xt[half_of(half), sixteen(i), :] = block.astype(BF16).reshape(16, 16, 128)

    def xt_block(half, i):
        return xt[half_of(half), sixteen(i), :].reshape(256, 128)

    def send_store(slot):
        def store(half, i, block):
            send[slot + half, sixteen(i)] = block.astype(BF16).reshape(16, 16, 128)

        return store

    def rest_block(half, i):
        return xt_rest[half_of(half), sixteen(i), :].reshape(256, 128)

    def fg_store(half, i, block):
        block = block + dot(swap[...], rest_block(half, i))
        for s in range(16):
            lanes = pl.ds(pl.multiple_of((i * 16 + s) * 128, 128), 128)
            fg_ref[half_of(half), lanes] = block[s * 16 : (s + 1) * 16]

    def forward(ws):
        outer = [dot(first[...], jnp.concatenate([xt[w], xt[w]], axis=0)) for w in ws]
        twisted = []
        for x in outer:
            re, im = x[:128], x[128:]
            c, s = cos[...], sin[...]
            twisted.append(
                jnp.concatenate([re * c + im * s, im * c - re * s], axis=1).astype(BF16)
            )
        return [dot(x, wide[0:256]) for x in twisted]

    def backward(ws, products, keep_rest=False):
        inner = [dot(x, wide[256:512]) for x in products]
        twisted = []
        for x in inner:
            re, im = x[:, :128], x[:, 128:]
            c, s = cos[...], sin[...]
            twisted.append(
                jnp.concatenate([re * c - im * s, re * s + im * c], axis=0).astype(BF16)
            )
        for w, x in zip(ws, twisted):
            y = dot(wide[1024:1152], x)
            xt[w] = y.astype(BF16)
            if keep_rest:
                xt_rest[w] = (y - y.astype(BF16).astype(F32)).astype(BF16)

    def product(x, y):
        xr, xi, yr, yi = x[:, :128], x[:, 128:], y[:, :128], y[:, 128:]
        return jnp.concatenate([xr * yr - xi * yi, xr * yi + xi * yr], axis=1).astype(BF16)

    def conj_product(x, y):
        xr, xi, yr, yi = x[:, :128], x[:, 128:], y[:, :128], y[:, 128:]
        return jnp.concatenate([xr * yr + xi * yi, xr * yi - xi * yr], axis=1).astype(BF16)

    def groups(half, body):
        @pl.loop(half * HALF // GROUP, (half + 1) * HALF // GROUP)
        def _(i):
            body([i * GROUP + j for j in range(GROUP)])

    def taps_step(ws):
        for w, x in zip(ws, forward(ws)):
            spec_h[w] = x

    def gated_step(ws):
        found = forward(ws)
        for w, x in zip(ws, found):
            spec_g[w] = x
        backward(ws, [product(x, spec_h[w]) for w, x in zip(ws, found)])

    def grad_step(ws):
        found = forward(ws)
        for w, x in zip(ws, found):
            spec_q[w] = x
        backward(ws, [conj_product(spec_h[w], x) for w, x in zip(ws, found)])

    def filter_step(ws):
        backward(ws, [conj_product(spec_g[w], spec_q[w]) for w in ws], keep_rest=True)

    for half in range(2):
        swap_blocks(half, taps_block, xt_store)
        groups(half, taps_step)
    for slot, step in ((0, gated_step), (2, grad_step)):
        for half in range(2):
            wait_recv(slot + half)
            swap_blocks(half, recv_block(slot), xt_store)
            groups(half, step)
            swap_blocks(half, xt_block, send_store(slot + 4))
            start_sends(slot + 4 + half)
    for half in range(2):
        groups(half, filter_step)
        swap_blocks(half, xt_block, fg_store)

    wait_recv(4)
    wait_recv(5)

    @pl.loop(0, C // 256 // UNROLL)
    def _(i):
        gate_out(i, wide[512:640, 0:128], recv.at[4], recv.at[5], [(qg_ref, g)])

    wait_recv(6)
    wait_recv(7)
    for slot in range(8):
        wait_send(slot)


def finish(
    qg, fg, back, k, v, qg_hbm, fg_hbm, kg_hbm, vg_hbm, kg, vg, sem
):
    copies = [
        pltpu.make_async_copy(fg, fg_hbm, sem.at[0]),
        pltpu.make_async_copy(qg, qg_hbm, sem.at[1]),
    ]
    for copy in copies:
        copy.start()
    rows = lax.broadcasted_iota(jnp.int32, (128, 128), 0)
    unit = (rows == lax.broadcasted_iota(jnp.int32, (128, 128), 1)).astype(F32).astype(BF16)
    steps = C // 256 // UNROLL
    for i in range(steps):
        gate_out(i, unit, back.at[0], back.at[1], [(kg, v), (vg, k)])
        cols = pl.ds(i * 256 * UNROLL, 256 * UNROLL)
        for j, (src, dst) in enumerate([(kg, kg_hbm), (vg, vg_hbm)]):
            copy = pltpu.make_async_copy(src.at[:, cols], dst.at[:, cols], sem.at[2 + 2 * i + j])
            copy.start()
            copies.append(copy)
    for copy in copies:
        copy.wait()


def local(queries, keys, values, grad_out, filter_param):
    wide, first, twist = make_tables()
    operands = (queries, keys, values, grad_out, filter_param.T, wide, first, twist)
    hbm = pl.BlockSpec(memory_space=pltpu.HBM)
    vmem = pl.BlockSpec(memory_space=pltpu.VMEM)
    rows = (N, C)
    out = pl.pallas_call(
        kernel,
        out_shape=[
            pltpu.VMEM(rows, BF16),
            pltpu.VMEM((W, N * N), F32),
            pltpu.VMEM((2, N, HALF, 128), BF16),
            pltpu.VMEM(rows, BF16),
            pltpu.VMEM(rows, BF16),
        ],
        in_specs=[hbm] * 8,
        out_specs=[vmem] * 5,
        scratch_shapes=[
            pltpu.VMEM(rows, BF16),
            pltpu.VMEM(rows, BF16),
            pltpu.VMEM((W, N * N), F32),
            pltpu.VMEM(wide.shape, BF16),
            pltpu.VMEM(first.shape, BF16),
            pltpu.VMEM(twist.shape, F32),
            pltpu.VMEM((8, N, HALF, 128), BF16),
            pltpu.VMEM((6, N, HALF, 128), BF16),
            pltpu.VMEM((W, 128, 128), BF16),
            pltpu.VMEM((W, 128, 128), BF16),
            pltpu.VMEM((W, 128, 256), F32),
            pltpu.VMEM((W, 128, 256), F32),
            pltpu.VMEM((W, 128, 256), F32),
            pltpu.SemaphoreType.DMA((8,)),
            pltpu.SemaphoreType.DMA((8,)),
            pltpu.SemaphoreType.DMA((8,)),
            pltpu.SemaphoreType.DMA((8,)),
        ],
        compiler_params=pltpu.CompilerParams(
            collective_id=0, has_side_effects=True, vmem_limit_bytes=40 << 20
        ),
        cost_estimate=pl.CostEstimate(flops=5 << 30, bytes_accessed=11 << 20, transcendentals=0),
    )(*[pltpu.with_memory_space_constraint(x, pltpu.HBM) for x in operands])
    query_grad, filter_grad, key_grad, value_grad = pl.pallas_call(
        finish,
        out_shape=[
            jax.ShapeDtypeStruct(rows, BF16),
            jax.ShapeDtypeStruct((W, N * N), F32),
            jax.ShapeDtypeStruct(rows, BF16),
            jax.ShapeDtypeStruct(rows, BF16),
        ],
        in_specs=[pl.BlockSpec(memory_space=pl.ANY)] * 2 + [vmem] * 3,
        out_specs=[hbm] * 4,
        scratch_shapes=[
            pltpu.VMEM(rows, BF16),
            pltpu.VMEM(rows, BF16),
            pltpu.SemaphoreType.DMA((2 + 2 * (C // 256 // UNROLL),)),
        ],
        compiler_params=pltpu.CompilerParams(vmem_limit_bytes=8 << 20),
    )(*out)
    return query_grad, key_grad, value_grad, filter_grad.T


def solution(mesh):
    split = P(("dp", "ctx"), None)
    channels = P(None, ("dp", "ctx"))
    return jax.shard_map(
        local,
        mesh=mesh,
        in_specs=(split, split, split, split, channels),
        out_specs=(split, split, split, channels),
        check_vma=False,
    )
```

```python
import functools
import math

import jax
import jax.numpy as jnp
import numpy as np
from jax import lax
from jax.experimental import pallas as pl
from jax.experimental.pallas import tpu as pltpu
from jax.sharding import PartitionSpec as P

MESH = pl.DeviceIdType.MESH
F32 = jnp.float32
BF16 = jnp.bfloat16
N = 128
W = 32
HALF = W // 2
C = N * W
GROUP = 4
UNROLL = 4
SWAP_UNROLL = 4


def make_tables():
    a = np.arange(128, dtype=np.float64)
    k = np.arange(128, dtype=np.float64)
    outer = 2.0 * np.pi * np.outer(k + 0.5, a) / 256.0
    first = np.concatenate([np.cos(outer), -np.sin(outer)], axis=0)
    last = first.T * (2.0 / 32768.0 / 128.0)
    inner = 2.0 * np.pi * (np.outer(a, a) % 128) / 128.0
    c, s = np.cos(inner), np.sin(inner)
    second = np.block([[c, -s], [s, c]])
    twist = 2.0 * np.pi * np.outer(k + 0.5, a) / 32768.0
    index = np.arange(256)
    swap = np.zeros((256, 256))
    swap[index, (index % 16) * 16 + index // 16] = 1.0
    first_high = first.astype(BF16).astype(np.float64)
    first = np.concatenate([first_high, first - first_high], axis=1)
    wide = np.concatenate([second, second.T, np.eye(256), swap, last], axis=0)
    return (
        jnp.asarray(wide.astype(np.float32), BF16),
        jnp.asarray(first.astype(np.float32), BF16),
        jnp.asarray(np.concatenate([np.cos(twist), np.sin(twist)], axis=0), F32),
    )


def dot(x, y):
    return lax.dot_general(x, y, (((1,), (0,)), ((), ())), preferred_element_type=F32)


def dot_nt(x, y):
    return lax.dot_general(x, y, (((1,), (1,)), ((), ())), preferred_element_type=F32)


def unit_matrix(size):
    rows = lax.broadcasted_iota(jnp.int32, (size, size), 0)
    cols = lax.broadcasted_iota(jnp.int32, (size, size), 1)
    return (rows == cols).astype(F32).astype(BF16)


def gate_out(i, unit, low, high, pairs):
    found = []
    for u in range(UNROLL):
        rows = pl.ds(pl.multiple_of((i * UNROLL + u) * 8, 8), 8)
        both = jnp.concatenate([low[rows], high[rows]], axis=1)
        found.append(dot_nt(unit, both.reshape(256, 128)))
    for u in range(UNROLL):
        cols = pl.ds(pl.multiple_of((i * UNROLL + u) * 256, 256), 256)
        for out_ref, gate in pairs:
            out_ref[:, cols] = (gate[:, cols].astype(F32) * found[u]).astype(BF16)


def kernel(
    q_hbm, k_hbm, v_hbm, g_hbm, taps_hbm, wide_hbm, first_hbm, twist_hbm,
    qg_ref, fg_ref, back, k, v,
    q, g, taps, wide, first, twist,
    send, recv, xt, xt_rest, spec_h, spec_g, spec_q,
    load_sem, send_sem, recv_sem, own_sem,
):
    dp, ctx = lax.axis_index("dp"), lax.axis_index("ctx")
    me = dp * 16 + ctx
    cx, cy, cz, cc = (dp % 2) * 2 + (ctx // 2) % 2, ctx // 4, dp // 2, ctx % 2

    loads = [
        pltpu.make_async_copy(src, dst, load_sem.at[i])
        for i, (src, dst) in enumerate(
            [(k_hbm, k), (v_hbm, v), (wide_hbm, wide), (q_hbm, q), (g_hbm, g),
             (first_hbm, first), (twist_hbm, twist), (taps_hbm, taps)]
        )
    ]
    for load in loads[:2]:
        load.start()

    xs = [(cx + r) % 4 for r in range(4)]
    x_dp = [x // 2 for x in xs]
    x_ctx = [(x % 2) * 2 for x in xs]
    y_ctx = [((cy + r) % 4) * 4 for r in range(4)]
    c_ctx = [cc, 1 - cc]

    def partners(visit):
        @pl.loop(0, 8)
        def _(m):
            z_dp = [((cz + m + r) % 4) * 2 for r in range(4)]
            far = m // 4
            c_now = [far + (1 - 2 * far) * c for c in c_ctx]
            for n in range(4):
                for r in range(4):
                    d = z_dp[(n + r) % 4] + x_dp[r]
                    e = y_ctx[(n + r) % 4] + x_ctx[r] + c_now[r % 2]
                    if n + r == 0:
                        pl.when(m > 0)(functools.partial(visit, d, e))
                    else:
                        visit(d, e)

    barrier = pltpu.get_barrier_semaphore()

    partners(
        lambda d, e: pl.semaphore_signal(barrier, inc=1, device_id=(d, e), device_id_type=MESH)
    )
    for load in loads[2:]:
        load.start()

    ident = unit_matrix(256)
    swap = wide.at[768:1024]

    def gate_in(left, right, slot):
        @pl.loop(0, C // 256 // UNROLL)
        def _(i):
            turned = []
            for u in range(UNROLL):
                cols = pl.ds(pl.multiple_of(i * (256 * UNROLL) + u * 256, 256), 256)
                gated = (left[:, cols].astype(F32) * right[:, cols].astype(F32)).astype(BF16)
                turned.append(dot_nt(ident, gated).astype(BF16))
            for u in range(UNROLL):
                block = turned[u].reshape(8, W, 128)
                rows = pl.ds(pl.multiple_of(i * (8 * UNROLL) + u * 8, 8), 8)
                send[slot, rows] = block[:, :HALF]
                send[slot + 1, rows] = block[:, HALF:]

    for load in loads[:2]:
        load.wait()
    gate_in(k, v, 0)
    pl.semaphore_wait(barrier, N - 1)

    def landing(slot):
        return recv.at[slot] if slot < 6 else back.at[slot - 6]

    def start_sends(slot):

        def visit(d, e):
            pltpu.make_async_remote_copy(
                src_ref=send.at[slot, d * 16 + e],
                dst_ref=landing(slot).at[me],
                send_sem=send_sem.at[slot],
                recv_sem=recv_sem.at[slot],
                device_id=(d, e),
                device_id_type=MESH,
            ).start()

        partners(visit)
        pltpu.make_async_copy(send.at[slot, me], landing(slot).at[me], own_sem.at[slot]).start()

    def wait_recv(slot):

        others = landing(slot).at[pl.ds(0, N - 1)]
        pltpu.make_async_copy(others, others, recv_sem.at[slot]).wait()
        pltpu.make_async_copy(send.at[slot, me], landing(slot).at[me], own_sem.at[slot]).wait()

    def wait_send(slot):

        others = send.at[slot, pl.ds(0, N - 1)]
        pltpu.make_async_copy(others, others, send_sem.at[slot]).wait()

    start_sends(0)
    start_sends(1)
    for load in loads[3:5]:
        load.wait()
    gate_in(g, q, 2)
    start_sends(2)
    start_sends(3)
    for load in loads[5:] + loads[2:3]:
        load.wait()

    cos, sin = twist.at[0:128], twist.at[128:256]

    def swap_blocks(half, load_block, store_block):
        @pl.loop(0, 8 // SWAP_UNROLL)
        def _(i):
            blocks = [i * SWAP_UNROLL + u for u in range(SWAP_UNROLL)]
            found = [dot(swap[...], load_block(half, block)) for block in blocks]
            for block, x in zip(blocks, found):
                store_block(half, block, x)

    def sixteen(i):
        return pl.ds(pl.multiple_of(i * 16, 16), 16)

    def half_of(half):
        return pl.ds(half * HALF, HALF)

    def recv_block(slot):
        return lambda half, i: recv[slot + half, sixteen(i)].reshape(256, 128)

    def taps_block(half, i):
        parts = []
        for s in range(16):
            lanes = pl.ds(pl.multiple_of((i * 16 + s) * 128, 128), 128)
            parts.append(taps[half_of(half), lanes])
        return jnp.concatenate(parts, axis=0).astype(BF16)

    def xt_store(half, i, block):
        xt[half_of(half), sixteen(i), :] = block.astype(BF16).reshape(16, 16, 128)

    def xt_block(half, i):
        return xt[half_of(half), sixteen(i), :].reshape(256, 128)

    def send_store(slot):
        def store(half, i, block):
            send[slot + half, sixteen(i)] = block.astype(BF16).reshape(16, 16, 128)

        return store

    def rest_block(half, i):
        return xt_rest[half_of(half), sixteen(i), :].reshape(256, 128)

    def fg_store(half, i, block):
        block = block + dot(swap[...], rest_block(half, i))
        for s in range(16):
            lanes = pl.ds(pl.multiple_of((i * 16 + s) * 128, 128), 128)
            fg_ref[half_of(half), lanes] = block[s * 16 : (s + 1) * 16]

    def forward(ws):
        outer = [dot(first[...], jnp.concatenate([xt[w], xt[w]], axis=0)) for w in ws]
        twisted = []
        for x in outer:
            re, im = x[:128], x[128:]
            c, s = cos[...], sin[...]
            twisted.append(
                jnp.concatenate([re * c + im * s, im * c - re * s], axis=1).astype(BF16)
            )
        return [dot(x, wide[0:256]) for x in twisted]

    def backward(ws, products, keep_rest=False):
        inner = [dot(x, wide[256:512]) for x in products]
        twisted = []
        for x in inner:
            re, im = x[:, :128], x[:, 128:]
            c, s = cos[...], sin[...]
            twisted.append(
                jnp.concatenate([re * c - im * s, re * s + im * c], axis=0).astype(BF16)
            )
        for w, x in zip(ws, twisted):
            y = dot(wide[1024:1152], x)
            xt[w] = y.astype(BF16)
            if keep_rest:
                xt_rest[w] = (y - y.astype(BF16).astype(F32)).astype(BF16)

    def product(x, y):
        xr, xi, yr, yi = x[:, :128], x[:, 128:], y[:, :128], y[:, 128:]
        return jnp.concatenate([xr * yr - xi * yi, xr * yi + xi * yr], axis=1).astype(BF16)

    def conj_product(x, y):
        xr, xi, yr, yi = x[:, :128], x[:, 128:], y[:, :128], y[:, 128:]
        return jnp.concatenate([xr * yr + xi * yi, xr * yi - xi * yr], axis=1).astype(BF16)

    def groups(half, body):
        @pl.loop(half * HALF // GROUP, (half + 1) * HALF // GROUP)
        def _(i):
            body([i * GROUP + j for j in range(GROUP)])

    def taps_step(ws):
        for w, x in zip(ws, forward(ws)):
            spec_h[w] = x

    def gated_step(ws):
        found = forward(ws)
        for w, x in zip(ws, found):
            spec_g[w] = x
        backward(ws, [product(x, spec_h[w]) for w, x in zip(ws, found)])

    def grad_step(ws):
        found = forward(ws)
        for w, x in zip(ws, found):
            spec_q[w] = x
        backward(ws, [conj_product(spec_h[w], x) for w, x in zip(ws, found)])

    def filter_step(ws):
        backward(ws, [conj_product(spec_g[w], spec_q[w]) for w in ws], keep_rest=True)

    for half in range(2):
        swap_blocks(half, taps_block, xt_store)
        groups(half, taps_step)
    for slot, step in ((0, gated_step), (2, grad_step)):
        for half in range(2):
            wait_recv(slot + half)
            swap_blocks(half, recv_block(slot), xt_store)
            groups(half, step)
            swap_blocks(half, xt_block, send_store(slot + 4))
            start_sends(slot + 4 + half)
    for half in range(2):
        groups(half, filter_step)
        swap_blocks(half, xt_block, fg_store)

    wait_recv(4)
    wait_recv(5)

    @pl.loop(0, C // 256 // UNROLL)
    def _(i):
        gate_out(i, wide[512:640, 0:128], recv.at[4], recv.at[5], [(qg_ref, g)])

    wait_recv(6)
    wait_recv(7)
    for slot in range(8):
        wait_send(slot)


def finish(
    qg, fg, back, k, v, qg_hbm, fg_hbm, kg_hbm, vg_hbm, kg, vg, sem
):
    copies = [
        pltpu.make_async_copy(fg, fg_hbm, sem.at[0]),
        pltpu.make_async_copy(qg, qg_hbm, sem.at[1]),
    ]
    for copy in copies:
        copy.start()
    unit = unit_matrix(128)
    steps = C // 256 // UNROLL
    for i in range(steps):
        gate_out(i, unit, back.at[0], back.at[1], [(kg, v), (vg, k)])
        cols = pl.ds(i * 256 * UNROLL, 256 * UNROLL)
        for j, (src, dst) in enumerate([(kg, kg_hbm), (vg, vg_hbm)]):
            copy = pltpu.make_async_copy(src.at[:, cols], dst.at[:, cols], sem.at[2 + 2 * i + j])
            copy.start()
            copies.append(copy)
    for copy in copies:
        copy.wait()


def local(queries, keys, values, grad_out, filter_param):
    wide, first, twist = make_tables()
    operands = (queries, keys, values, grad_out, filter_param.T, wide, first, twist)
    hbm = pl.BlockSpec(memory_space=pltpu.HBM)
    vmem = pl.BlockSpec(memory_space=pltpu.VMEM)
    rows = (N, C)
    out = pl.pallas_call(
        kernel,
        out_shape=[
            pltpu.VMEM(rows, BF16),
            pltpu.VMEM((W, N * N), F32),
            pltpu.VMEM((2, N, HALF, 128), BF16),
            pltpu.VMEM(rows, BF16),
            pltpu.VMEM(rows, BF16),
        ],
        in_specs=[hbm] * 8,
        out_specs=[vmem] * 5,
        scratch_shapes=[
            pltpu.VMEM(rows, BF16),
            pltpu.VMEM(rows, BF16),
            pltpu.VMEM((W, N * N), F32),
            pltpu.VMEM(wide.shape, BF16),
            pltpu.VMEM(first.shape, BF16),
            pltpu.VMEM(twist.shape, F32),
            pltpu.VMEM((8, N, HALF, 128), BF16),
            pltpu.VMEM((6, N, HALF, 128), BF16),
            pltpu.VMEM((W, 128, 128), BF16),
            pltpu.VMEM((W, 128, 128), BF16),
            pltpu.VMEM((W, 128, 256), F32),
            pltpu.VMEM((W, 128, 256), F32),
            pltpu.VMEM((W, 128, 256), F32),
            pltpu.SemaphoreType.DMA((8,)),
            pltpu.SemaphoreType.DMA((8,)),
            pltpu.SemaphoreType.DMA((8,)),
            pltpu.SemaphoreType.DMA((8,)),
        ],
        compiler_params=pltpu.CompilerParams(
            collective_id=0, has_side_effects=True, vmem_limit_bytes=40 << 20
        ),
        cost_estimate=pl.CostEstimate(flops=5 << 30, bytes_accessed=11 << 20, transcendentals=0),
    )(*[pltpu.with_memory_space_constraint(x, pltpu.HBM) for x in operands])
    query_grad, filter_grad, key_grad, value_grad = pl.pallas_call(
        finish,
        out_shape=[
            jax.ShapeDtypeStruct(rows, BF16),
            jax.ShapeDtypeStruct((W, N * N), F32),
            jax.ShapeDtypeStruct(rows, BF16),
            jax.ShapeDtypeStruct(rows, BF16),
        ],
        in_specs=[pl.BlockSpec(memory_space=pl.ANY)] * 2 + [vmem] * 3,
        out_specs=[hbm] * 4,
        scratch_shapes=[
            pltpu.VMEM(rows, BF16),
            pltpu.VMEM(rows, BF16),
            pltpu.SemaphoreType.DMA((2 + 2 * (C // 256 // UNROLL),)),
        ],
        compiler_params=pltpu.CompilerParams(vmem_limit_bytes=8 << 20),
    )(*out)
    return query_grad, key_grad, value_grad, filter_grad.T


def solution(mesh):
    split = P(("dp", "ctx"), None)
    channels = P(None, ("dp", "ctx"))
    return jax.shard_map(
        local,
        mesh=mesh,
        in_specs=(split, split, split, split, channels),
        out_specs=(split, split, split, channels),
        check_vma=False,
    )
```
